256 devices in a mesh: dp: 32 (over x_hi, z, core), expert: 8 (over x_lo, y).
Axes of the slice: x: 4 (x_hi: 2, x_lo: 2; x = x_hi * 2 + x_lo), y: 4, z: 8, core: 2. Of those that a mesh axis runs over, the one named last changes fastest.
Arguments:
- tokens: bfloat16 [32768, 2048], P(('dp', 'expert')), may hold values from -24 to 24
- cotangent: bfloat16 [32768, 2048], P(('dp', 'expert')), may hold values from -6 to 6
- probs: bfloat16 [32768, 2], P(('dp', 'expert')), may hold values from 0.19921875 to 1
- routes: int32 [32768, 2], P(('dp', 'expert')), may hold values from 0 to 7, all different within a row; in each aligned block of 128 rows (0 to 127, 128 to 255, ...) at most 40 rows name the same one
- live: int32 [512], P(('dp', 'expert')), may hold values 0 or 1
- slot_map: int32 [8], replicated, may hold values from 0 to 7, each once
- w_gate: bfloat16 [8, 2048, 768], P('expert'), may hold values from -0.125 to 0.125
- w_up: bfloat16 [8, 2048, 768], P('expert'), may hold values from -0.125 to 0.125
- w_down: bfloat16 [8, 768, 2048], P('expert'), may hold values from -0.21875 to 0.21875
Outputs:
- input_grad: bfloat16 [32768, 2048], P(('dp', 'expert'))
- prob_grad: bfloat16 [32768, 2], P(('dp', 'expert'))
- grad_gate: float32 [8, 2048, 768], P('expert', 'dp')
- grad_up: float32 [8, 2048, 768], P('expert', 'dp')
- grad_down: float32 [8, 768, 2048], P('expert', None, 'dp')
The draws below stay inside these ranges and needn't reach their ends.
Inputs may be any that keep to these rules, and one draw needn't show every extreme that they name: `routes`: the tokens of one device name each expert in at most 40 pairs; some expert reaches 40 on some device. `slot_map`: each slot is named once.
All inputs are finite; a program needn't handle non-finite values. No bound on the sum of `live` on one device may be relied on, other than what follows from the above.
Results may differ from the reference program's by a relative error of at most 0.019.
Values may be sent and summed in bfloat16 or wider, within the bound.
A program may use at most 128 MiB of HBM per device.

```python
import math
import jax
import jax.numpy as jnp
import numpy as np
from jax import lax

D = 2048
FF = 768
TOP = 2
TOK_DEV = 128
SAMPLE_LEN = 64
EXPERTS = 8
TOKENS = 32768
CAP = 40
N_DP = 32
N_EXPERT = 8


def with_ends(drawn, stream_key, least, top_value):
    longest = drawn.shape.index(max(drawn.shape))
    spots = []
    for shift in (0, 1):
        where = [jax.random.randint(jax.random.fold_in(stream_key, axis), (), 0, length) for axis, length in enumerate(drawn.shape)]
        where[longest] = (where[longest] + shift) % drawn.shape[longest]
        spots.append(tuple(where))
    return drawn.at[spots[0]].set(least).at[spots[1]].set(top_value)


def raised(entries, own_key, source, target, blocks, factor):
    def block_of(axis_at):
        return (jnp.arange(entries.shape[axis_at]) // (entries.shape[axis_at] // blocks)).reshape((-1,) + (1,) * (entries.ndim - 1 - axis_at))

    near = jax.random.permutation(own_key, blocks)[block_of(target)]
    far = (block_of(target) + blocks // 2) % blocks
    return jnp.where((block_of(source) == near) | (block_of(source) == far), factor * entries, entries)


def steps_of(stream_key, dims, split, low, largest):
    loudness, own = 1.0, jax.random.fold_in(stream_key, 6)
    for dim, shards_of in split:
        steps = jnp.exp(jax.random.uniform(jax.random.fold_in(own, dim), (shards_of,), jnp.float32, low / len(split), largest / len(split)))
        loudness = loudness * jnp.repeat(steps, dims[dim] // shards_of).reshape([-1 if axis == dim else 1 for axis in range(len(dims))])
    return loudness


def assign_block(key, own, number, rows, amount, top, most, lean):
    order = jax.random.permutation(key, amount)
    packed, common = shares(amount, rows * top, most, lean, True), shares(amount, rows * top, most, lean, False)
    places = jnp.arange(amount)

    def named(lengths, offset_by):
        used = int((lengths > 0).sum())
        fixed = max(1, used // 4)
        moved = fixed + (places - fixed + offset_by * (used - fixed)) % max(1, amount - fixed)
        return jnp.zeros((amount,), jnp.int32).at[order[jnp.where(places < fixed, places, moved)]].set(jnp.asarray(lengths, jnp.int32))

    lengths = jnp.where(number % 4 == 0, named(packed, number // 4), named(common, number - number // 4 - 1))
    mixed = jax.random.permutation(jax.random.fold_in(own, 3), amount)
    source_of, sink = mixed[0:amount // 2 * 2:2], mixed[1:amount // 2 * 2:2]
    margin = jnp.minimum(lengths[source_of] - 1, most - lengths[sink]) // 2
    margin = jnp.where((source_of == order[0]) | (sink == order[0]) | (lengths[sink] == 0), 0, jnp.maximum(margin, 0))
    moved = jax.random.randint(jax.random.fold_in(own, 4), (amount // 2,), 0, 1 << 20) % (margin + 1)
    lengths = lengths.at[source_of].add(-moved).at[sink].add(moved)
    labels = jnp.searchsorted(jnp.cumsum(lengths), jnp.arange(rows * top), side="right").astype(jnp.int32)
    grid = labels.reshape(top, rows).T
    grid = grid[jax.random.permutation(jax.random.fold_in(own, 1), rows)]
    offset_by = jax.random.randint(jax.random.fold_in(own, 2), (rows, 1), 0, top)
    return jnp.take_along_axis(grid, (jnp.arange(top)[None, :] + offset_by) % top, axis=1)


def shares(amount, total, bound, skew, full):
    loads = [(1 << 20) // math.isqrt(standing ** skew) + 1 for standing in range(1, amount + 1)]
    largest = bound if full else min(bound, max(-(-total // amount), total * loads[0] // sum(loads)))
    least = 1 if total - largest >= amount - 1 else 0
    holding, spare = [largest] + [least] * (amount - 1), total - largest - least * (amount - 1)
    while spare > 0:
        candidates = [i for i in range(1, amount) if holding[i] < largest] or [i for i in range(1, amount) if holding[i] < bound]
        pool, left = sum([loads[i] for i in candidates]), spare
        for i in candidates:
            more = min(bound - holding[i], max(1, left * loads[i] // pool), spare)
            holding[i] = holding[i] + more
            spare = spare - more
    return np.array(holding)


def gaussian(stream_key, extent, spread, most, split=(), kind=jnp.bfloat16):
    drawn = jax.random.normal(stream_key, extent, jnp.float32) * spread
    if len(split) > 0:
        drawn = steps_of(stream_key, extent, split, -0.22, 0.18) * drawn
    return jnp.clip(drawn, min=-most, max=most).astype(kind)


def bell_draw_with(rng, shape, width, reach, split, heavy, kind=jnp.bfloat16):
    entries = width * jax.random.normal(rng, shape, jnp.float32)
    if split:
        entries = entries * steps_of(rng, shape, split, -0.22, 0.18)
    return jnp.clip(raised(entries, jax.random.fold_in(rng, 3), *heavy), -reach, reach).astype(kind)


def setup_inputs(seed: int = 0) -> dict:
    seeds = jax.random.split(jax.random.key(seed), 10)
    tokens = bell_draw_with(seeds[0], (TOKENS, D), 1.0, 24.0, ((0, 256),), (0, 1, 256, 6.0))
    cotangent = gaussian(seeds[1], (TOKENS, D), 1.0, 6.0, ((0, 256),))
    probs = jnp.clip(0.19921875 + 0.80078125 * jax.random.uniform(seeds[2], (TOKENS, TOP), jnp.float32) ** steps_of(seeds[2], (TOKENS, TOP), ((0, 256),), -0.2, 0.2), 0.19921875, 1.0).astype(jnp.bfloat16)
    routes_keys = jax.random.split(jax.random.fold_in(seeds[3], 1), TOKENS // TOK_DEV)
    routes_turns = jax.random.permutation(jax.random.fold_in(seeds[3], 3), TOKENS // TOK_DEV)
    routes = jax.vmap(lambda own, number: assign_block(jax.random.fold_in(seeds[3], 2), own, number, TOK_DEV, EXPERTS, TOP, CAP, 2))(routes_keys, routes_turns).reshape((TOKENS, TOP))
    live = with_ends((jax.random.randint(seeds[4], (TOKENS // SAMPLE_LEN,), 0, 4) < 3).astype(jnp.int32), jax.random.fold_in(seeds[4], 1), 0, 1)
    slot_map = jax.random.permutation(seeds[5], EXPERTS).astype(jnp.int32)
    w_gate = gaussian(seeds[6], (EXPERTS, D, FF), D ** -0.5, 0.125, ((0, 8),))
    w_up = gaussian(seeds[7], (EXPERTS, D, FF), D ** -0.5, 0.125, ((0, 8),))
    w_down = gaussian(seeds[8], (EXPERTS, FF, D), FF ** -0.5, 0.21875, ((0, 8),))
    return {"tokens": tokens, "cotangent": cotangent, "probs": probs, "routes": routes, "live": live, "slot_map": slot_map, "w_gate": w_gate, "w_up": w_up, "w_down": w_down}


def reference(tokens, cotangent, probs, routes, live, slot_map, w_gate, w_up, w_down):
    brows = N_EXPERT * TOK_DEV
    limit = N_EXPERT * CAP
    x3 = tokens.reshape(N_DP, brows, D)
    dy3 = cotangent.reshape(N_DP, brows, D)
    p3 = probs.reshape(N_DP, brows, TOP)
    r3 = routes.reshape(N_DP, brows, TOP)
    l3 = live.reshape(N_DP, brows // SAMPLE_LEN)

    def block_step(carry, item):
        xb, dyb, pb, rb, lb = item
        alive = jnp.repeat(lb, SAMPLE_LEN, total_repeat_length=brows)
        owner = slot_map[rb].reshape(-1)
        pair_tok = jnp.arange(brows * TOP, dtype=jnp.int32) // TOP
        pair_live = alive[pair_tok] == 1
        prob_flat = pb.reshape(-1).astype(jnp.float32)
        pair_sum = jnp.zeros((brows * TOP, D), jnp.float32)
        prob_sum = jnp.zeros((brows * TOP,), jnp.float32)
        grads_gate, grads_up, grads_down = [], [], []
        for slot in range(EXPERTS):
            hit = (owner == slot) & pair_live
            index = jnp.nonzero(hit, size=limit, fill_value=0)[0].astype(jnp.int32)
            valid = jnp.arange(limit, dtype=jnp.int32) < jnp.sum(hit.astype(jnp.int32))
            keep = valid.astype(jnp.float32)[:, None]
            rows_x = (xb[pair_tok[index]].astype(jnp.float32) * keep).astype(jnp.bfloat16)
            rows_dy = (dyb[pair_tok[index]].astype(jnp.float32) * keep).astype(jnp.bfloat16)
            weight = prob_flat[index] * valid.astype(jnp.float32)
            gate = jnp.dot(rows_x, w_gate[slot], preferred_element_type=jnp.float32)
            up = jnp.dot(rows_x, w_up[slot], preferred_element_type=jnp.float32)
            sig = jax.nn.sigmoid(gate)
            hidden = (gate * sig * up).astype(jnp.bfloat16)
            expert_out = jnp.dot(hidden, w_down[slot], preferred_element_type=jnp.float32)
            prob_part = jnp.sum(expert_out * rows_dy.astype(jnp.float32), -1).astype(jnp.bfloat16)
            scaled = (weight[:, None] * rows_dy.astype(jnp.float32)).astype(jnp.bfloat16)
            hidden_grad = jnp.dot(scaled, w_down[slot].T, preferred_element_type=jnp.float32)
            gate_grad = (hidden_grad * up * sig * (1.0 + gate * (1.0 - sig))).astype(jnp.bfloat16)
            up_grad = (hidden_grad * gate * sig).astype(jnp.bfloat16)
            pair = (jnp.dot(gate_grad, w_gate[slot].T, preferred_element_type=jnp.float32)
                    + jnp.dot(up_grad, w_up[slot].T, preferred_element_type=jnp.float32)).astype(jnp.bfloat16)
            pair_sum = pair_sum.at[index].add(pair.astype(jnp.float32))
            prob_sum = prob_sum.at[index].add(prob_part.astype(jnp.float32))
            grads_gate.append(jnp.dot(rows_x.T, gate_grad, preferred_element_type=jnp.float32))
            grads_up.append(jnp.dot(rows_x.T, up_grad, preferred_element_type=jnp.float32))
            grads_down.append(jnp.dot(hidden.T, scaled, preferred_element_type=jnp.float32))
        parts = (jnp.stack(grads_gate), jnp.stack(grads_up), jnp.stack(grads_down))
        rounded = tuple(lax.optimization_barrier(part.astype(jnp.bfloat16)).astype(jnp.float32) for part in parts)
        new_carry = tuple(total + part for total, part in zip(carry, rounded))
        input_grad = jnp.sum(pair_sum.reshape(brows, TOP, D), 1).astype(jnp.bfloat16)
        prob_grad = prob_sum.reshape(brows, TOP).astype(jnp.bfloat16)
        return new_carry, (input_grad, prob_grad)

    start = (jnp.zeros((EXPERTS, D, FF), jnp.float32), jnp.zeros((EXPERTS, D, FF), jnp.float32),
             jnp.zeros((EXPERTS, FF, D), jnp.float32))
    totals, outs = lax.scan(block_step, start, (x3, dy3, p3, r3, l3))
    input_grad = outs[0].reshape(N_DP * brows, D)
    prob_grad = outs[1].reshape(N_DP * brows, TOP)
    return input_grad, prob_grad, totals[0], totals[1], totals[2]
```

```python
import functools

import jax
import jax.numpy as jnp
from jax import lax
from jax.experimental import pallas as pl
from jax.experimental.pallas import tpu as pltpu
from jax.sharding import PartitionSpec as P

MESH = pl.DeviceIdType.MESH
NZ = 8


def contract_rows(left, right):
    return lax.dot_general(
        left, right, (((0,), (0,)), ((), ())), preferred_element_type=jnp.float32
    )


def contract_cols(left, right):
    return lax.dot_general(
        left, right, (((1,), (1,)), ((), ())), preferred_element_type=jnp.float32
    )


def reduce_kernel(g0, g1, g2, o0, o1, o2, sib, ring, xbuf, sib_s, sib_r, ring_s, ring_r, x_s, x_r):
    dp = lax.axis_index("dp")
    ex = lax.axis_index("expert")
    xh, z, c = dp // 16, (dp // 2) % NZ, dp % 2
    up = (xh * 16 + ((z + 1) % NZ) * 2 + c, ex)
    down = (xh * 16 + ((z + NZ - 1) % NZ) * 2 + c, ex)
    sibling = (xh * 16 + z * 2 + (1 - c), ex)
    across = ((1 - xh) * 16 + z * 2 + c, ex)
    grads, outs = (g0, g1, g2), (o0, o1, o2)

    barrier = pltpu.get_barrier_semaphore()
    for peer in (up, down, sibling, across):
        pl.semaphore_signal(barrier, inc=1, device_id=peer, device_id_type=MESH)
    pl.semaphore_wait(barrier, 4)

    def chunk(d, s):
        return (z + 2 * NZ - 1 - s) % NZ if d == 0 else (z + 1 + s) % NZ

    def sib_copy(m, d, s):
        at = chunk(d, s)
        return pltpu.make_async_remote_copy(
            src_ref=grads[m].at[d, at, 1 - c],
            dst_ref=sib.at[m, d, at],
            send_sem=sib_s.at[m, d, s],
            recv_sem=sib_r.at[m, d, s],
            device_id=sibling,
            device_id_type=MESH,
        )

    def ring_copy(m, d, s):
        return pltpu.make_async_remote_copy(
            src_ref=ring.at[m, d, s],
            dst_ref=ring.at[m, d, s + 1],
            send_sem=ring_s.at[m, d, s],
            recv_sem=ring_r.at[m, d, s],
            device_id=up if d == 0 else down,
            device_id_type=MESH,
        )

    def x_copy(m):
        return pltpu.make_async_remote_copy(
            src_ref=ring.at[m, 1 - xh, NZ - 1],
            dst_ref=xbuf.at[m],
            send_sem=x_s.at[m],
            recv_sem=x_r.at[m],
            device_id=across,
            device_id_type=MESH,
        )

    def own(m, d, at):
        return grads[m][d, at, c].astype(jnp.float32) + sib[m, d, at].astype(jnp.float32)

    @pl.loop(0, NZ)
    def _(s):
        for m in range(3):
            for d in range(2):
                sib_copy(m, d, s).start()

    for m in range(3):
        for d in range(2):
            sib_copy(m, d, 0).wait()
            ring[m, d, 0] = own(m, d, chunk(d, 0)).astype(jnp.bfloat16)
            ring_copy(m, d, 0).start()

    @pl.loop(1, NZ - 1)
    def _(s):
        for m in range(3):
            for d in range(2):
                sib_copy(m, d, s).wait()
                ring_copy(m, d, s - 1).wait()
                ring[m, d, s] = (
                    ring[m, d, s].astype(jnp.float32) + own(m, d, chunk(d, s))
                ).astype(jnp.bfloat16)
                ring_copy(m, d, s).start()

    last = NZ - 1
    for m in range(3):
        for d in range(2):
            sib_copy(m, d, last).wait()
            ring_copy(m, d, last - 1).wait()
        ring[m, 1 - xh, last] = (
            ring[m, 1 - xh, last].astype(jnp.float32) + own(m, 1 - xh, z)
        ).astype(jnp.bfloat16)
        x_copy(m).start()
    for m in range(3):
        x_copy(m).wait()
        outs[m][...] = (
            ring[m, xh, last].astype(jnp.float32)
            + own(m, xh, z)
            + xbuf[m].astype(jnp.float32)
        )


def reduce_all(g0, g1, g2):
    rows, cols = 64, g0.shape[1]
    parts = tuple(g.reshape(2, NZ, 2, rows, cols) for g in (g0, g1, g2))
    return pl.pallas_call(
        reduce_kernel,
        out_shape=[jax.ShapeDtypeStruct((rows, cols), jnp.float32)] * 3,
        in_specs=[pl.BlockSpec(memory_space=pltpu.VMEM)] * 3,
        out_specs=[pl.BlockSpec(memory_space=pltpu.VMEM)] * 3,
        scratch_shapes=[
            pltpu.VMEM((3, 2, NZ, rows, cols), jnp.bfloat16),
            pltpu.VMEM((3, 2, NZ, rows, cols), jnp.bfloat16),
            pltpu.VMEM((3, rows, cols), jnp.bfloat16),
            pltpu.SemaphoreType.DMA((3, 2, NZ)),
            pltpu.SemaphoreType.DMA((3, 2, NZ)),
            pltpu.SemaphoreType.DMA((3, 2, NZ - 1)),
            pltpu.SemaphoreType.DMA((3, 2, NZ - 1)),
            pltpu.SemaphoreType.DMA((3,)),
            pltpu.SemaphoreType.DMA((3,)),
        ],
        compiler_params=pltpu.CompilerParams(
            collective_id=0, has_side_effects=True, vmem_limit_bytes=48 * 2**20
        ),
        name="reduce_grads",
    )(*parts)


def shards(tokens, cotangent, probs, routes, live, slot_map, w_gate, w_up, w_down):
    rows, top = routes.shape
    width = tokens.shape[1]
    groups = lax.axis_size("expert")
    experts = slot_map.shape[0]
    cap = min(rows, rows * top * 5 // (4 * experts))
    slots = groups * cap
    alive = jnp.repeat(live, rows // live.shape[0])
    chosen = routes[:, :, None] == jnp.arange(experts, dtype=jnp.int32)[None, None, :]
    owner = jnp.sum(jnp.where(chosen, slot_map[None, None, :], 0), -1).reshape(-1)
    pair_live = jnp.repeat(alive, top) == 1
    taken = (
        (owner[:, None] == jnp.arange(groups, dtype=jnp.int32)[None, :]) & pair_live[:, None]
    ).astype(jnp.int32)
    before = jnp.cumsum(taken, 0) - taken
    position = jnp.sum(before * taken, 1)
    target = jnp.where(pair_live, owner * cap + position, -1)
    pick = (target[None, :] == jnp.arange(slots, dtype=jnp.int32)[:, None]).astype(jnp.float32)
    by_token = jnp.sum(pick.reshape(slots, rows, top), 2).astype(jnp.bfloat16)
    send_x = (
        jnp.dot(by_token, tokens, preferred_element_type=jnp.float32)
        .astype(jnp.bfloat16)
        .reshape(groups, cap, width)
    )
    send_dy = (
        jnp.dot(by_token, cotangent, preferred_element_type=jnp.float32)
        .astype(jnp.bfloat16)
        .reshape(groups, cap, width)
    )
    send_p = (
        jnp.sum(pick * probs.reshape(-1).astype(jnp.float32)[None, :], 1)
        .astype(jnp.bfloat16)
        .reshape(groups, cap)
    )
    gate_w = w_gate[0]
    up_w = w_up[0]
    down_w = w_down[0]
    got_x, got_p = (
        lax.all_to_all(send_x, "expert", split_axis=0, concat_axis=0, tiled=True),
        lax.all_to_all(send_p, "expert", split_axis=0, concat_axis=0, tiled=True),
    )
    rows_x = got_x.reshape(slots, width)
    gate = jnp.dot(rows_x, gate_w, preferred_element_type=jnp.float32)
    up = jnp.dot(rows_x, up_w, preferred_element_type=jnp.float32)
    got_dy = lax.all_to_all(send_dy, "expert", split_axis=0, concat_axis=0, tiled=True)
    rows_dy = got_dy.reshape(slots, width)
    weight = got_p.reshape(slots).astype(jnp.float32)
    sig = jax.nn.sigmoid(gate)
    hidden = (gate * sig * up).astype(jnp.bfloat16)
    expert_out = jnp.dot(hidden, down_w, preferred_element_type=jnp.float32)
    prob_part = jnp.sum(expert_out * rows_dy.astype(jnp.float32), -1).astype(jnp.bfloat16)
    scaled = (weight[:, None] * rows_dy.astype(jnp.float32)).astype(jnp.bfloat16)
    grad_down = contract_rows(scaled, hidden)
    hidden_grad = contract_cols(scaled, down_w)
    gate_grad = (hidden_grad * up * sig * (1.0 + gate * (1.0 - sig))).astype(jnp.bfloat16)
    up_grad = (hidden_grad * gate * sig).astype(jnp.bfloat16)
    pair = (contract_cols(gate_grad, gate_w) + contract_cols(up_grad, up_w)).astype(jnp.bfloat16)
    back, back_p = (
        lax.all_to_all(
            pair.reshape(groups, cap, width), "expert", split_axis=0, concat_axis=0, tiled=True
        ),
        lax.all_to_all(
            prob_part.reshape(groups, cap), "expert", split_axis=0, concat_axis=0, tiled=True
        ),
    )
    grad_gate = contract_rows(rows_x, gate_grad)
    grad_up = contract_rows(rows_x, up_grad)
    down_share, gate_share, up_share = reduce_all(
        grad_down.astype(jnp.bfloat16),
        grad_gate.astype(jnp.bfloat16),
        grad_up.astype(jnp.bfloat16),
    )
    input_grad = contract_rows(by_token, back.reshape(slots, width)).astype(jnp.bfloat16)
    prob_grad = (
        jnp.sum(pick * back_p.reshape(slots).astype(jnp.float32)[:, None], 0)
        .reshape(rows, top)
        .astype(jnp.bfloat16)
    )
    return (input_grad, prob_grad, gate_share[None], up_share[None], down_share.T[None])


def solution(mesh):
    return jax.shard_map(
        shards,
        mesh=mesh,
        in_specs=(
            P(("dp", "expert"), None),
            P(("dp", "expert"), None),
            P(("dp", "expert"), None),
            P(("dp", "expert"), None),
            P(("dp", "expert")),
            P(),
            P("expert", None, None),
            P("expert", None, None),
            P("expert", None, None),
        ),
        out_specs=(
            P(("dp", "expert"), None),
            P(("dp", "expert"), None),
            P("expert", "dp", None),
            P("expert", "dp", None),
            P("expert", None, "dp"),
        ),
        check_vma=False,
    )
```

```python
import jax
import jax.numpy as jnp
from jax import lax
from jax.experimental import pallas as pl
from jax.experimental.pallas import tpu as pltpu
from jax.sharding import PartitionSpec as P

MESH = pl.DeviceIdType.MESH
F32, BF16 = jnp.float32, jnp.bfloat16
NZ = 8
NE = 8
TOK = 128
WIDE = 2048
HALF = 1024
FF = 768
MAIN = 32
REST = 8
ROWS = NE * (MAIN + REST)
LAST = NZ - 1


def mm(a, b):
    return jnp.dot(a, b, preferred_element_type=F32)


def mm_tn(a, b):
    return lax.dot_general(a, b, (((0,), (0,)), ((), ())), preferred_element_type=F32)


def mm_nt(a, b):
    return lax.dot_general(a, b, (((1,), (1,)), ((), ())), preferred_element_type=F32)


def cols_at(start, size):
    return pl.ds(pl.multiple_of(start, size), size)


def one_hot(hit):
    return jnp.where(hit, 1.0, 0.0).astype(BF16)


def layer_kernel(
    slot_ref, live_ref, routes_ref, probs_ref, tok_ref, cot_ref, wg_hbm, wu_hbm, wd_hbm,
    in_ref, pg_ref, o_down, o_gate, o_up,
    wg, wu, wd, w_sem,
    pick, pick_a, pick_b, pick48,
    sx, sxt, sdy, sdyt, sp, x, xt, dy, dyt, prob,
    hid, phid, act1, act2, gg, ug, pp,
    pair, pairt, sbp, back, backt, bp,
    grads, sib, ring, xbuf,
    a2a_s, a2a_r, sib_s, sib_r, ring_s, ring_r, x_s, x_r,
):
    dp = lax.axis_index("dp")
    me = lax.axis_index("expert")
    xh, z, c = dp // 16, (dp // 2) % NZ, dp % 2
    up = (xh * 16 + ((z + 1) % NZ) * 2 + c, me)
    down = (xh * 16 + ((z + NZ - 1) % NZ) * 2 + c, me)
    sibling = (xh * 16 + z * 2 + (1 - c), me)
    across = ((1 - xh) * 16 + z * 2 + c, me)

    weights = [
        pltpu.make_async_copy(src, dst, w_sem.at[i])
        for i, (src, dst) in enumerate(((wg_hbm, wg), (wu_hbm, wu), (wd_hbm, wd)))
    ]
    for w in weights:
        w.start()

    barrier = pltpu.get_barrier_semaphore()
    for peer in (up, down, sibling, across):
        pl.semaphore_signal(barrier, inc=1, device_id=peer, device_id_type=MESH)
    for k in range(1, NE):
        pl.semaphore_signal(
            barrier, inc=1, device_id=(dp, (me + k) % NE), device_id_type=MESH
        )

    slot_iota = lax.broadcasted_iota(jnp.int32, (NE, TOK), 0)
    lane = lax.broadcasted_iota(jnp.int32, (1, TOK), 1)
    alive = jnp.where(lane < TOK // 2, live_ref[0], live_ref[1]) == 1
    owners = []
    for k in range(2):
        r = routes_ref[k : k + 1, :]
        o = jnp.zeros((1, TOK), jnp.int32)
        for e in range(NE):
            o = jnp.where(r == e, slot_ref[e], o)
        owners.append(jnp.where(alive, o, -1))
    taken = sum(jnp.where(slot_iota == o, 1.0, 0.0) for o in owners).astype(BF16)
    earlier = lax.broadcasted_iota(jnp.int32, (TOK, TOK), 0) < lax.broadcasted_iota(
        jnp.int32, (TOK, TOK), 1
    )
    before = mm(taken, one_hot(earlier))
    mains, rests, alls = [], [], []
    for o in owners:
        pos = jnp.sum(jnp.where(slot_iota == o, before, 0.0), 0, keepdims=True).astype(jnp.int32)
        mains.append(jnp.where((o >= 0) & (pos < MAIN), o * MAIN + pos, -1))
        rests.append(jnp.where((o >= 0) & (pos >= MAIN), o * 2 * REST + pos - MAIN, -1))
        alls.append(jnp.where(o >= 0, o * 48 + pos, -1))
    row = lax.broadcasted_iota(jnp.int32, (NE * MAIN, TOK), 0)
    pick[...] = one_hot((row == mains[0]) | (row == mains[1]))
    row = lax.broadcasted_iota(jnp.int32, (NE * 2 * REST, TOK), 0)
    pick_a[...] = one_hot((row == rests[0]) | (row == rests[1]))
    low = row - REST
    pick_b[...] = one_hot(
        ((low == rests[0]) & (rests[0] >= 0)) | ((low == rests[1]) & (rests[1] >= 0))
    )

    def dispatch(src, main, rest):
        @pl.loop(0, 4)
        def _(n):
            cols = cols_at(n * 512, 512)
            main[:, cols] = mm(pick[...], src[:, cols]).astype(BF16)

        @pl.loop(0, 2)
        def _(n):
            cols = cols_at(n * 512, 512)
            more = cols_at(HALF + n * 512, 512)
            rest[:, cols] = (
                mm(pick_a[...], src[:, cols]) + mm(pick_b[...], src[:, more])
            ).astype(BF16)

    def piece(ref, kind, e):
        if kind % 3 == 0:
            return ref.at[pl.ds(pl.multiple_of(e * MAIN, MAIN), MAIN)]
        if kind % 3 == 1:
            return ref.at[pl.ds(pl.multiple_of(e * 2 * REST, 2 * REST), 2 * REST)]
        return ref.at[e]

    exchanged = (
        (sx, x), (sxt, xt), (sp, prob),
        (sdy, dy), (sdyt, dyt), None,
        (pair, back), (pairt, backt), (sbp, bp),
    )

    def exchange(kind, k):
        src, dst = exchanged[kind]
        to = (me + k) % NE
        return pltpu.make_async_remote_copy(
            src_ref=piece(src, kind, to),
            dst_ref=piece(dst, kind, me),
            send_sem=a2a_s.at[kind, k],
            recv_sem=a2a_r.at[kind, k],
            device_id=(dp, to),
            device_id_type=MESH,
        )

    def start_all(kinds):
        @pl.loop(1, NE)
        def _(k):
            for kind in kinds:
                exchange(kind, k).start()

    def keep_own(kinds):
        for kind in kinds:
            src, dst = exchanged[kind]
            if kind % 3 == 2:
                dst[me] = src[me]
            else:
                size = MAIN if kind % 3 == 0 else 2 * REST
                rows = pl.ds(pl.multiple_of(me * size, size), size)
                dst[rows, :] = src[rows, :]

    def wait_sent(kinds):
        @pl.loop(1, NE)
        def _(k):
            for kind in kinds:
                exchange(kind, k).wait_send()

    def wait_got(kinds):
        @pl.loop(1, NE)
        def _(k):
            for kind in kinds:
                exchange(kind, k).wait_recv()

    dispatch(tok_ref, sx, sxt)
    pl.semaphore_wait(barrier, 4 + NE - 1)
    start_all((0, 1))
    row = lax.broadcasted_iota(jnp.int32, (NE * 48, TOK), 0)
    total = jnp.zeros((NE * 48, 1), F32)
    for k in range(2):
        hit = jnp.where(row == alls[k], 1.0, 0.0)
        pick48[k] = hit
        total += jnp.sum(hit * probs_ref[k : k + 1, :], 1, keepdims=True)
    sp[...] = jnp.broadcast_to(total, (NE * 48, 128)).astype(BF16).reshape(NE, 48, 128)
    keep_own((0, 1, 2))
    dispatch(cot_ref, sdy, sdyt)
    keep_own((3, 4))
    wait_sent((0, 1))
    start_all((3, 4, 2))

    part = lax.broadcasted_iota(jnp.int32, (NE * REST, NE * 2 * REST), 0)
    from_row = lax.broadcasted_iota(jnp.int32, (NE * REST, NE * 2 * REST), 1)
    first = (part // REST) * 2 * REST + part % REST
    take_a, take_b = one_hot(from_row == first), one_hot(from_row == first + REST)

    def join(main, rest):
        rows = pl.ds(NE * MAIN, NE * REST)

        @pl.loop(0, 2)
        def _(n):
            cols = cols_at(n * 512, 512)
            half = rest[:, cols]
            main[rows, cols] = mm(take_a, half).astype(BF16)
            main[rows, cols_at(HALF + n * 512, 512)] = mm(take_b, half).astype(BF16)

    wait_got((0, 1))
    join(x, xt)
    weights[0].wait()
    weights[1].wait()

    @pl.loop(0, FF // 256)
    def _(n):
        cols = cols_at(n * 256, 256)
        gate = mm(x[...], wg[:, cols])
        u = mm(x[...], wu[:, cols])
        sig = jax.nn.sigmoid(gate)
        gs = gate * sig
        hid[:, cols] = (gs * u).astype(BF16)
        act1[:, cols] = u * sig * (1.0 + gate * (1.0 - sig))
        act2[:, cols] = gs

    weights[2].wait()
    wait_got((2,))
    p_all = prob[...].astype(F32)
    weight = jnp.concatenate(
        [
            p_all[:, :MAIN].reshape(NE * MAIN, 128),
            p_all[:, MAIN : MAIN + REST].reshape(NE * REST, 128),
        ],
        0,
    )[:, :1]
    phid[...] = (weight * hid[...].astype(F32)).astype(BF16)
    wait_got((3, 4))
    join(dy, dyt)

    def chunk(d, s):
        return (z + 2 * NZ - 1 - s) % NZ if d == 0 else (z + 1 + s) % NZ

    def sib_copy(m, d, s):
        at = chunk(d, s)
        return pltpu.make_async_remote_copy(
            src_ref=grads.at[m, d, at, 1 - c],
            dst_ref=sib.at[m, d, at],
            send_sem=sib_s.at[m, d, s],
            recv_sem=sib_r.at[m, d, s],
            device_id=sibling,
            device_id_type=MESH,
        )

    def ring_copy(m, d, s):
        return pltpu.make_async_remote_copy(
            src_ref=ring.at[m, d, s],
            dst_ref=ring.at[m, d, s + 1],
            send_sem=ring_s.at[m, d, s],
            recv_sem=ring_r.at[m, d, s],
            device_id=up if d == 0 else down,
            device_id_type=MESH,
        )

    def x_copy(m):
        return pltpu.make_async_remote_copy(
            src_ref=ring.at[m, 1 - xh, LAST],
            dst_ref=xbuf.at[m],
            send_sem=x_s.at[m],
            recv_sem=x_r.at[m],
            device_id=across,
            device_id_type=MESH,
        )

    def own(m, d, at):
        return grads[m, d, at, c].astype(F32) + sib[m, d, at].astype(F32)

    def make_grads(left, rights):
        @pl.loop(0, NZ)
        def _(s):
            lhs = jnp.concatenate(
                [
                    left[:, cols_at(chunk(0, s) * 128, 128)],
                    left[:, cols_at(HALF + chunk(1, s) * 128, 128)],
                ],
                1,
            )
            for m, right in rights:
                out = mm_tn(lhs, right[...]).astype(BF16)
                for d in range(2):
                    grads[m, d, chunk(d, s)] = out[d * 128 : d * 128 + 128].reshape(2, 64, FF)
                    sib_copy(m, d, s).start()

    def ring_start(m):
        for d in range(2):
            sib_copy(m, d, 0).wait()
            ring[m, d, 0] = own(m, d, chunk(d, 0)).astype(BF16)
            ring_copy(m, d, 0).start()

    def ring_step(m, s):
        for d in range(2):
            sib_copy(m, d, s).wait()
            ring_copy(m, d, s - 1).wait()
            ring[m, d, s] = (ring[m, d, s].astype(F32) + own(m, d, chunk(d, s))).astype(BF16)
            ring_copy(m, d, s).start()

    def ring_end(m):
        for d in range(2):
            sib_copy(m, d, LAST).wait()
            ring_copy(m, d, LAST - 1).wait()
        ring[m, 1 - xh, LAST] = (
            ring[m, 1 - xh, LAST].astype(F32) + own(m, 1 - xh, z)
        ).astype(BF16)
        x_copy(m).start()

    make_grads(dy, ((0, phid),))
    ring_start(0)

    pp[...] = jnp.zeros_like(pp)

    @pl.loop(0, FF // 256)
    def _(n):
        cols = cols_at(n * 256, 256)
        dyw = mm_nt(dy[...], wd[cols, :])
        pp[...] += jnp.sum(hid[:, cols].astype(F32) * dyw, 1, keepdims=True)
        hg = dyw * weight
        gg[:, cols] = (hg * act1[:, cols]).astype(BF16)
        ug[:, cols] = (hg * act2[:, cols]).astype(BF16)

    ring_step(0, 1)
    make_grads(x, ((1, gg), (2, ug)))
    ring_start(1)
    ring_start(2)
    ring_step(0, 2)

    @pl.loop(0, WIDE // 256)
    def _(n):
        cols = cols_at(n * 256, 256)
        pair[:, cols] = (mm_nt(gg[...], wg[cols, :]) + mm_nt(ug[...], wu[cols, :])).astype(BF16)

    rows = pl.ds(NE * MAIN, NE * REST)

    @pl.loop(0, 2)
    def _(n):
        cols = cols_at(n * 512, 512)
        pairt[:, cols] = (
            mm_tn(take_a, pair[rows, cols])
            + mm_tn(take_b, pair[rows, cols_at(HALF + n * 512, 512)])
        ).astype(BF16)

    part = jnp.broadcast_to(pp[...], (ROWS, 128))
    sbp[:, :MAIN] = part[: NE * MAIN].reshape(NE, MAIN, 128).astype(BF16)
    sbp[:, MAIN:] = jnp.concatenate(
        [part[NE * MAIN :].reshape(NE, REST, 128), jnp.zeros((NE, REST, 128), F32)], 1
    ).astype(BF16)
    start_all((6, 7, 8))
    keep_own((6, 7, 8))

    @pl.loop(1, 5)
    def _(s):
        ring_step(1, s)
        ring_step(2, s)
        ring_step(0, s + 2)

    ring_step(1, 5)
    ring_step(2, 5)
    ring_end(0)
    ring_step(1, 6)
    ring_step(2, 6)

    wait_got((6, 7, 8))

    @pl.loop(0, 2)
    def _(n):
        cols = cols_at(n * 512, 512)
        more = cols_at(HALF + n * 512, 512)
        in_ref[:, cols] = (
            mm_tn(pick[...], back[:, cols]) + mm_tn(pick_a[...], backt[:, cols])
        ).astype(BF16)
        in_ref[:, more] = (
            mm_tn(pick[...], back[:, more]) + mm_tn(pick_b[...], backt[:, cols])
        ).astype(BF16)

    parts = bp[...].astype(F32).reshape(NE * 48, 128)
    for k in range(2):
        pg_ref[k : k + 1, :] = jnp.sum(pick48[k] * parts, 0, keepdims=True)

    ring_end(1)
    ring_end(2)
    for m, out in enumerate((o_down, o_gate, o_up)):
        x_copy(m).wait()
        out[...] = ring[m, xh, LAST].astype(F32) + own(m, xh, z) + xbuf[m].astype(F32)
    wait_sent((2, 3, 4, 6, 7, 8))


def layer(slot_map, live, routes, probs, tokens, cotangent, wg, wu, wd):
    vmem, smem = pl.BlockSpec(memory_space=pltpu.VMEM), pl.BlockSpec(memory_space=pltpu.SMEM)
    anywhere = pl.BlockSpec(memory_space=pl.ANY)
    dma = pltpu.SemaphoreType.DMA
    return pl.pallas_call(
        layer_kernel,
        out_shape=[
            jax.ShapeDtypeStruct((TOK, WIDE), BF16),
            jax.ShapeDtypeStruct((2, TOK), F32),
        ]
        + [jax.ShapeDtypeStruct((64, FF), F32)] * 3,
        in_specs=[smem, smem, vmem, vmem, vmem, vmem, anywhere, anywhere, anywhere],
        out_specs=[vmem] * 5,
        scratch_shapes=[
            pltpu.VMEM((WIDE, FF), BF16),
            pltpu.VMEM((WIDE, FF), BF16),
            pltpu.VMEM((FF, WIDE), BF16),
            dma((3,)),
            pltpu.VMEM((NE * MAIN, TOK), BF16),
            pltpu.VMEM((NE * 2 * REST, TOK), BF16),
            pltpu.VMEM((NE * 2 * REST, TOK), BF16),
            pltpu.VMEM((2, NE * 48, TOK), F32),
            pltpu.VMEM((NE * MAIN, WIDE), BF16),
            pltpu.VMEM((NE * 2 * REST, HALF), BF16),
            pltpu.VMEM((NE * MAIN, WIDE), BF16),
            pltpu.VMEM((NE * 2 * REST, HALF), BF16),
            pltpu.VMEM((NE, 48, 128), BF16),
            pltpu.VMEM((ROWS, WIDE), BF16),
            pltpu.VMEM((NE * 2 * REST, HALF), BF16),
            pltpu.VMEM((ROWS, WIDE), BF16),
            pltpu.VMEM((NE * 2 * REST, HALF), BF16),
            pltpu.VMEM((NE, 48, 128), BF16),
            pltpu.VMEM((ROWS, FF), BF16),
            pltpu.VMEM((ROWS, FF), BF16),
            pltpu.VMEM((ROWS, FF), F32),
            pltpu.VMEM((ROWS, FF), F32),
            pltpu.VMEM((ROWS, FF), BF16),
            pltpu.VMEM((ROWS, FF), BF16),
            pltpu.VMEM((ROWS, 1), F32),
            pltpu.VMEM((ROWS, WIDE), BF16),
            pltpu.VMEM((NE * 2 * REST, HALF), BF16),
            pltpu.VMEM((NE, 48, 128), BF16),
            pltpu.VMEM((NE * MAIN, WIDE), BF16),
            pltpu.VMEM((NE * 2 * REST, HALF), BF16),
            pltpu.VMEM((NE, 48, 128), BF16),
            pltpu.VMEM((3, 2, NZ, 2, 64, FF), BF16),
            pltpu.VMEM((3, 2, NZ, 64, FF), BF16),
            pltpu.VMEM((3, 2, NZ, 64, FF), BF16),
            pltpu.VMEM((3, 64, FF), BF16),
            dma((9, NE)),
            dma((9, NE)),
            dma((3, 2, NZ)),
            dma((3, 2, NZ)),
            dma((3, 2, NZ - 1)),
            dma((3, 2, NZ - 1)),
            dma((3,)),
            dma((3,)),
        ],
        compiler_params=pltpu.CompilerParams(
            collective_id=0, has_side_effects=True, vmem_limit_bytes=56 * 2**20
        ),
        cost_estimate=pl.CostEstimate(
            flops=9 * 2 * ROWS * WIDE * FF, bytes_accessed=12 * 2**20, transcendentals=ROWS * FF
        ),
        name="moe_layer",
    )(slot_map, live, routes, probs, tokens, cotangent, wg, wu, wd)


def shards(tokens, cotangent, probs, routes, live, slot_map, w_gate, w_up, w_down):
    input_grad, prob_grad, down_share, gate_share, up_share = layer(
        slot_map,
        live,
        routes.T,
        probs.T.astype(F32),
        tokens,
        cotangent,
        w_gate[0],
        w_up[0],
        w_down[0],
    )
    return (
        input_grad,
        prob_grad.T.astype(BF16),
        gate_share[None],
        up_share[None],
        down_share.T[None],
    )


def solution(mesh):
    tok = P(("dp", "expert"), None)
    return jax.shard_map(
        shards,
        mesh=mesh,
        in_specs=(
            tok, tok, tok, tok,
            P(("dp", "expert")),
            P(),
            P("expert", None, None),
            P("expert", None, None),
            P("expert", None, None),
        ),
        out_specs=(
            tok,
            tok,
            P("expert", "dp", None),
            P("expert", "dp", None),
            P("expert", None, "dp"),
        ),
        check_vma=False,
    )
```

```python
import jax
import jax.numpy as jnp
from jax import lax
from jax.experimental import pallas as pl
from jax.experimental.pallas import tpu as pltpu
from jax.sharding import PartitionSpec as P

MESH = pl.DeviceIdType.MESH
F32, BF16 = jnp.float32, jnp.bfloat16
NZ = 8
NE = 8
TOK = 128
WIDE = 2048
HALF = 1024
FF = 768
MAIN = 32
REST = 8
ROWS = NE * (MAIN + REST)
LAST = NZ - 1
GROUP = 2
FIRST = NZ // GROUP


def mm(a, b):
    return jnp.dot(a, b, preferred_element_type=F32)


def mm_tn(a, b):
    return lax.dot_general(a, b, (((0,), (0,)), ((), ())), preferred_element_type=F32)


def mm_nt(a, b):
    return lax.dot_general(a, b, (((1,), (1,)), ((), ())), preferred_element_type=F32)


def cols_at(start, size):
    return pl.ds(pl.multiple_of(start, size), size)


def one_hot(hit):
    return jnp.where(hit, 1.0, 0.0).astype(BF16)


def layer_kernel(
    slot_ref, live_ref, routes_ref, probs_ref, tok_hbm, cot_hbm, wg_hbm, wu_hbm, wd_hbm,
    in_ref, pg_ref, o_down, o_gate, o_up,
    tok_ref, cot_ref, wg, wu, wd, w_sem,
    pick, pick_a, pick_b, pick48,
    sx, sxt, sdy, sdyt, sp, x, xt, dy, dyt, prob, turned,
    hid, phid, act1, act2, dyw, gg, ug,
    pair, pairt, sbp, back, backt, bp,
    grads, sib, ring, xbuf,
    a2a_s, a2a_r, dy_s, dy_r, sib_s, sib_r, ring_s, ring_r, x_s, x_r,
):
    dp = lax.axis_index("dp")
    me = lax.axis_index("expert")
    xh, z, c = dp // 16, (dp // 2) % NZ, dp % 2
    up = (xh * 16 + ((z + 1) % NZ) * 2 + c, me)
    down = (xh * 16 + ((z + NZ - 1) % NZ) * 2 + c, me)
    sibling = (xh * 16 + z * 2 + (1 - c), me)
    across = ((1 - xh) * 16 + z * 2 + c, me)

    loads = [
        pltpu.make_async_copy(src, dst, w_sem.at[i])
        for i, (src, dst) in enumerate(
            (
                (tok_hbm, tok_ref),
                (cot_hbm, cot_ref),
                (wg_hbm, wg),
                (wu_hbm, wu),
                (wd_hbm, wd),
            )
        )
    ]
    loads[0].start()

    def partner(k):
        return ((me // 4 + 1 - k // 4) % 2) * 4 + (me % 4 + k % 4 + k // 4) % 4

    barrier = pltpu.get_barrier_semaphore()
    for peer in (up, down, sibling, across):
        pl.semaphore_signal(barrier, inc=1, device_id=peer, device_id_type=MESH)
    for k in range(NE - 1):
        pl.semaphore_signal(
            barrier, inc=1, device_id=(dp, partner(k)), device_id_type=MESH
        )
    for load in loads[1:]:
        load.start()

    slot_iota = lax.broadcasted_iota(jnp.int32, (NE, TOK), 0)
    lane = lax.broadcasted_iota(jnp.int32, (1, TOK), 1)
    alive = jnp.where(lane < TOK // 2, live_ref[0], live_ref[1]) == 1
    owners = []
    for k in range(2):
        r = routes_ref[k : k + 1, :]
        o = jnp.zeros((1, TOK), jnp.int32)
        for e in range(NE):
            o = jnp.where(r == e, slot_ref[e], o)
        owners.append(jnp.where(alive, o, -1))
    taken = sum(jnp.where(slot_iota == o, 1.0, 0.0) for o in owners).astype(BF16)
    earlier = lax.broadcasted_iota(jnp.int32, (TOK, TOK), 0) < lax.broadcasted_iota(
        jnp.int32, (TOK, TOK), 1
    )
    before = mm(taken, one_hot(earlier))
    mains, rests, alls = [], [], []
    for o in owners:
        pos = jnp.sum(jnp.where(slot_iota == o, before, 0.0), 0, keepdims=True).astype(jnp.int32)
        mains.append(jnp.where((o >= 0) & (pos < MAIN), o * MAIN + pos, -1))
        rests.append(jnp.where((o >= 0) & (pos >= MAIN), o * 2 * REST + pos - MAIN, -1))
        alls.append(jnp.where(o >= 0, o * 48 + pos, -1))
    row = lax.broadcasted_iota(jnp.int32, (NE * MAIN, TOK), 0)
    pick[...] = one_hot((row == mains[0]) | (row == mains[1]))
    row = lax.broadcasted_iota(jnp.int32, (NE * 2 * REST, TOK), 0)
    pick_a[...] = one_hot((row == rests[0]) | (row == rests[1]))
    low = row - REST
    pick_b[...] = one_hot(
        ((low == rests[0]) & (rests[0] >= 0)) | ((low == rests[1]) & (rests[1] >= 0))
    )

    def dispatch():
        @pl.loop(0, 4)
        def _(n):
            cols = cols_at(n * 512, 512)
            sx[:, cols] = mm(pick[...], tok_ref[:, cols]).astype(BF16)

        @pl.loop(0, 2)
        def _(n):
            cols = cols_at(n * 512, 512)
            more = cols_at(HALF + n * 512, 512)
            sxt[:, cols] = (
                mm(pick_a[...], tok_ref[:, cols]) + mm(pick_b[...], tok_ref[:, more])
            ).astype(BF16)

    def chunk(d, s):
        return (z + 2 * NZ - 1 - s) % NZ if d == 0 else (z + 1 + s) % NZ

    def step_cols(s):
        return cols_at(chunk(0, s) * 128, 128), cols_at(HALF + chunk(1, s) * 128, 128)

    def both(ref, s):
        a, b = step_cols(s)
        return jnp.concatenate([ref[:, a], ref[:, b]], 1)

    def dispatch_cot():
        @pl.loop(0, NZ)
        def _(s):
            a, b = step_cols(s)
            sdy[s] = mm(pick[...], both(cot_ref, s)).astype(BF16)
            sdyt[s] = (mm(pick_a[...], cot_ref[:, a]) + mm(pick_b[...], cot_ref[:, b])).astype(
                BF16
            )

    def piece(ref, kind, e):
        if kind % 3 == 0:
            return ref.at[pl.ds(pl.multiple_of(e * MAIN, MAIN), MAIN)]
        if kind % 3 == 1:
            return ref.at[pl.ds(pl.multiple_of(e * 2 * REST, 2 * REST), 2 * REST)]
        return ref.at[e]

    exchanged = (
        (sx, x), (sxt, xt), (sp, prob),
        None, None, None,
        (pair, back), (pairt, backt), (sbp, bp),
    )

    def exchange(kind, k):
        src, dst = exchanged[kind]
        to = partner(k)
        return pltpu.make_async_remote_copy(
            src_ref=piece(src, kind, to),
            dst_ref=piece(dst, kind, me),
            send_sem=a2a_s.at[kind, k],
            recv_sem=a2a_r.at[kind, k],
            device_id=(dp, to),
            device_id_type=MESH,
        )

    def start_all(kinds):
        @pl.loop(0, NE - 1)
        def _(k):
            for kind in kinds:
                exchange(kind, k).start()

    def keep_own(kinds):
        for kind in kinds:
            src, dst = exchanged[kind]
            if kind % 3 == 2:
                dst[me] = src[me]
            else:
                size = MAIN if kind % 3 == 0 else 2 * REST
                rows = pl.ds(pl.multiple_of(me * size, size), size)
                dst[rows, :] = src[rows, :]

    def wait_sent(kinds):
        @pl.loop(0, NE - 1)
        def _(k):
            for kind in kinds:
                exchange(kind, k).wait_send()

    def wait_got(kinds):
        @pl.loop(0, NE - 1)
        def _(k):
            for kind in kinds:
                exchange(kind, k).wait_recv()

    def dy_copy(kind, g, k):
        to = partner(k)
        steps = pl.ds(g * GROUP, GROUP)
        src, dst, size = ((sdy, dy, MAIN), (sdyt, dyt, 2 * REST))[kind]
        return pltpu.make_async_remote_copy(
            src_ref=src.at[steps, pl.ds(pl.multiple_of(to * size, size), size)],
            dst_ref=dst.at[steps, pl.ds(pl.multiple_of(me * size, size), size)],
            send_sem=dy_s.at[kind, g, k],
            recv_sem=dy_r.at[kind, g, k],
            device_id=(dp, to),
            device_id_type=MESH,
        )

    loads[0].wait()
    dispatch()
    pl.semaphore_wait(barrier, 4 + NE - 1)
    start_all((0, 1))
    row = lax.broadcasted_iota(jnp.int32, (NE * 48, TOK), 0)
    total = jnp.zeros((NE * 48, 1), F32)
    for k in range(2):
        hit = jnp.where(row == alls[k], 1.0, 0.0)
        pick48[k] = hit
        total += jnp.sum(hit * probs_ref[k : k + 1, :].astype(F32), 1, keepdims=True)
    sp[...] = jnp.broadcast_to(total, (NE * 48, 128)).astype(BF16).reshape(NE, 48, 128)
    keep_own((0, 1, 2))
    loads[1].wait()
    dispatch_cot()
    for size, src, dst in ((MAIN, sdy, dy), (2 * REST, sdyt, dyt)):
        rows = pl.ds(pl.multiple_of(me * size, size), size)
        dst[:, rows, :] = src[:, rows, :]
    start_all((2,))

    @pl.loop(0, NZ // GROUP)
    def _(g):
        @pl.loop(0, NE - 1)
        def _(k):
            for kind in range(2):
                dy_copy(kind, g, k).start()

    part = lax.broadcasted_iota(jnp.int32, (NE * REST, NE * 2 * REST), 0)
    from_row = lax.broadcasted_iota(jnp.int32, (NE * REST, NE * 2 * REST), 1)
    first = (part // REST) * 2 * REST + part % REST
    take_a, take_b = one_hot(from_row == first), one_hot(from_row == first + REST)

    rest_rows = pl.ds(NE * MAIN, NE * REST)
    wait_got((0, 1))

    @pl.loop(0, 2)
    def _(n):
        cols = cols_at(n * 512, 512)
        half = xt[:, cols]
        x[rest_rows, cols] = mm(take_a, half).astype(BF16)
        x[rest_rows, cols_at(HALF + n * 512, 512)] = mm(take_b, half).astype(BF16)

    loads[2].wait()
    loads[3].wait()

    @pl.loop(0, FF // 256)
    def _(n):
        cols = cols_at(n * 256, 256)
        gate = mm(x[...], wg[:, cols])
        u = mm(x[...], wu[:, cols])
        sig = jax.nn.sigmoid(gate)
        gs = gate * sig
        hid[:, cols] = (gs * u).astype(BF16)
        act1[:, cols] = u * sig * (1.0 + gate * (1.0 - sig))
        act2[:, cols] = gs

    loads[4].wait()
    wait_got((2,))
    p_all = prob[...].astype(F32)
    weight = jnp.concatenate(
        [
            p_all[:, :MAIN].reshape(NE * MAIN, 128),
            p_all[:, MAIN : MAIN + REST].reshape(NE * REST, 128),
        ],
        0,
    )[:, :1]
    phid[...] = (weight * hid[...].astype(F32)).astype(BF16)

    def sib_copy(m, d, s):
        at = chunk(d, s)
        return pltpu.make_async_remote_copy(
            src_ref=grads.at[m, d, at, 1 - c],
            dst_ref=sib.at[m, d, at],
            send_sem=sib_s.at[m, d, s],
            recv_sem=sib_r.at[m, d, s],
            device_id=sibling,
            device_id_type=MESH,
        )

    def ring_copy(m, d, s):
        return pltpu.make_async_remote_copy(
            src_ref=ring.at[m, d, s],
            dst_ref=ring.at[m, d, s + 1],
            send_sem=ring_s.at[m, d, s],
            recv_sem=ring_r.at[m, d, s],
            device_id=up if d == 0 else down,
            device_id_type=MESH,
        )

    def x_copy(m):
        return pltpu.make_async_remote_copy(
            src_ref=ring.at[m, 1 - xh, LAST],
            dst_ref=xbuf.at[m],
            send_sem=x_s.at[m],
            recv_sem=x_r.at[m],
            device_id=across,
            device_id_type=MESH,
        )

    def own(m, d, at):
        return grads[m, d, at, c].astype(F32) + sib[m, d, at].astype(F32)

    def put_grads(m, s, out):
        for d in range(2):
            grads[m, d, chunk(d, s)] = out[d * 128 : d * 128 + 128].reshape(2, 64, FF)
            sib_copy(m, d, s).start()

    def ring_start(m):
        for d in range(2):
            sib_copy(m, d, 0).wait()
            ring[m, d, 0] = own(m, d, chunk(d, 0)).astype(BF16)
            ring_copy(m, d, 0).start()

    def ring_step(m, s):
        for d in range(2):
            sib_copy(m, d, s).wait()
            ring_copy(m, d, s - 1).wait()
            ring[m, d, s] = (ring[m, d, s].astype(F32) + own(m, d, chunk(d, s))).astype(BF16)
            ring_copy(m, d, s).start()

    def ring_end(m):
        for d in range(2):
            sib_copy(m, d, LAST).wait()
            ring_copy(m, d, LAST - 1).wait()
        ring[m, 1 - xh, LAST] = (
            ring[m, 1 - xh, LAST].astype(F32) + own(m, 1 - xh, z)
        ).astype(BF16)
        x_copy(m).start()

    dyw[...] = jnp.zeros_like(dyw)
    for g in range(NZ // GROUP):

        @pl.loop(0, NE - 1)
        def _(k):
            for kind in range(2):
                dy_copy(kind, g, k).wait_recv()

        @pl.loop(g * GROUP, g * GROUP + GROUP)
        def _(s):
            half = dyt[s]
            dy[s, rest_rows, :128] = mm(take_a, half).astype(BF16)
            dy[s, rest_rows, 128:] = mm(take_b, half).astype(BF16)
            put_grads(0, s, mm_tn(dy[s], phid[...]).astype(BF16))

        @pl.loop(g * GROUP, g * GROUP + GROUP)
        def _(s):
            dyw[...] += mm_nt(dy[s], both(wd, s))
            turned[s] = both(x, s).T

        if g == 0:
            ring_start(0)
        elif g < FIRST - 1:
            ring_step(0, g)

    total = jnp.zeros((ROWS, 1), F32)
    for n in range(FF // 256):
        cols = pl.ds(n * 256, 256)
        part = dyw[:, cols]
        total += jnp.sum(hid[:, cols].astype(F32) * part, 1, keepdims=True)
        hg = part * weight
        gg[:, cols] = (hg * act1[:, cols]).astype(BF16)
        ug[:, cols] = (hg * act2[:, cols]).astype(BF16)

    for m, right in ((1, gg), (2, ug)):

        @pl.loop(0, NZ)
        def _(s):
            put_grads(m, s, mm(turned[s], right[...]).astype(BF16))

        ring_start(m)

    def pair_cols(n):
        cols = cols_at(n * 256, 256)
        pair[:, cols] = (mm_nt(gg[...], wg[cols, :]) + mm_nt(ug[...], wu[cols, :])).astype(BF16)

    pair_cols(0)
    ring_step(0, FIRST - 1)
    pair_cols(1)

    @pl.loop(1, 3)
    def _(s):
        ring_step(1, s)
        pair_cols(3 * s - 1)
        ring_step(2, s)
        pair_cols(3 * s)
        ring_step(0, s + FIRST - 1)
        pair_cols(3 * s + 1)

    @pl.loop(0, 2)
    def _(n):
        cols = cols_at(n * 512, 512)
        pairt[:, cols] = (
            mm_tn(take_a, pair[rest_rows, cols])
            + mm_tn(take_b, pair[rest_rows, cols_at(HALF + n * 512, 512)])
        ).astype(BF16)

    part = jnp.broadcast_to(total, (ROWS, 128))
    sbp[:, :MAIN] = part[: NE * MAIN].reshape(NE, MAIN, 128).astype(BF16)
    sbp[:, MAIN:] = jnp.concatenate(
        [part[NE * MAIN :].reshape(NE, REST, 128), jnp.zeros((NE, REST, 128), F32)], 1
    ).astype(BF16)
    start_all((6, 7, 8))
    keep_own((6, 7, 8))

    ring_step(1, 3)
    ring_step(2, 3)
    ring_step(0, LAST - 1)

    for s in range(LAST - FIRST + 1, LAST):
        ring_step(1, s)
        ring_step(2, s)
        if s == LAST - FIRST + 1:
            ring_end(0)

    wait_got((6, 7, 8))

    @pl.loop(0, 2)
    def _(n):
        cols = cols_at(n * 512, 512)
        more = cols_at(HALF + n * 512, 512)
        in_ref[:, cols] = (
            mm_tn(pick[...], back[:, cols]) + mm_tn(pick_a[...], backt[:, cols])
        ).astype(BF16)
        in_ref[:, more] = (
            mm_tn(pick[...], back[:, more]) + mm_tn(pick_b[...], backt[:, cols])
        ).astype(BF16)

    parts = bp[...].astype(F32).reshape(NE * 48, 128)
    for k in range(2):
        pg_ref[k : k + 1, :] = jnp.sum(pick48[k] * parts, 0, keepdims=True).astype(BF16)

    ring_end(1)
    ring_end(2)
    for m, out in enumerate((o_down, o_gate, o_up)):
        x_copy(m).wait()
        out[...] = ring[m, xh, LAST].astype(F32) + own(m, xh, z) + xbuf[m].astype(F32)
    wait_sent((0, 1, 2, 6, 7, 8))

    @pl.loop(0, NZ // GROUP)
    def _(g):
        @pl.loop(0, NE - 1)
        def _(k):
            for kind in range(2):
                dy_copy(kind, g, k).wait_send()


def hand_over(*refs):
    half = len(refs) // 2
    for src, dst in zip(refs[:half], refs[half:]):
        dst[...] = src[...]


def layer(slot_map, live, routes, probs, tokens, cotangent, wg, wu, wd):
    vmem, smem = pl.BlockSpec(memory_space=pltpu.VMEM), pl.BlockSpec(memory_space=pltpu.SMEM)
    anywhere = pl.BlockSpec(memory_space=pl.ANY)
    dma = pltpu.SemaphoreType.DMA
    shapes = [
        jax.ShapeDtypeStruct((TOK, WIDE), BF16),
        jax.ShapeDtypeStruct((2, TOK), BF16),
    ] + [jax.ShapeDtypeStruct((64, FF), F32)] * 3
    results = pl.pallas_call(
        layer_kernel,
        out_shape=shapes,
        in_specs=[smem, smem, vmem, vmem] + [anywhere] * 5,
        out_specs=[vmem] * 5,
        scratch_shapes=[
            pltpu.VMEM((TOK, WIDE), BF16),
            pltpu.VMEM((TOK, WIDE), BF16),
            pltpu.VMEM((WIDE, FF), BF16),
            pltpu.VMEM((WIDE, FF), BF16),
            pltpu.VMEM((FF, WIDE), BF16),
            dma((5,)),
            pltpu.VMEM((NE * MAIN, TOK), BF16),
            pltpu.VMEM((NE * 2 * REST, TOK), BF16),
            pltpu.VMEM((NE * 2 * REST, TOK), BF16),
            pltpu.VMEM((2, NE * 48, TOK), F32),
            pltpu.VMEM((NE * MAIN, WIDE), BF16),
            pltpu.VMEM((NE * 2 * REST, HALF), BF16),
            pltpu.VMEM((NZ, NE * MAIN, 256), BF16),
            pltpu.VMEM((NZ, NE * 2 * REST, 128), BF16),
            pltpu.VMEM((NE, 48, 128), BF16),
            pltpu.VMEM((ROWS, WIDE), BF16),
            pltpu.VMEM((NE * 2 * REST, HALF), BF16),
            pltpu.VMEM((NZ, ROWS, 256), BF16),
            pltpu.VMEM((NZ, NE * 2 * REST, 128), BF16),
            pltpu.VMEM((NE, 48, 128), BF16),
            pltpu.VMEM((NZ, 256, ROWS), BF16),
            pltpu.VMEM((ROWS, FF), BF16),
            pltpu.VMEM((ROWS, FF), BF16),
            pltpu.VMEM((ROWS, FF), F32),
            pltpu.VMEM((ROWS, FF), F32),
            pltpu.VMEM((ROWS, FF), F32),
            pltpu.VMEM((ROWS, FF), BF16),
            pltpu.VMEM((ROWS, FF), BF16),
            pltpu.VMEM((ROWS, WIDE), BF16),
            pltpu.VMEM((NE * 2 * REST, HALF), BF16),
            pltpu.VMEM((NE, 48, 128), BF16),
            pltpu.VMEM((NE * MAIN, WIDE), BF16),
            pltpu.VMEM((NE * 2 * REST, HALF), BF16),
            pltpu.VMEM((NE, 48, 128), BF16),
            pltpu.VMEM((3, 2, NZ, 2, 64, FF), BF16),
            pltpu.VMEM((3, 2, NZ, 64, FF), BF16),
            pltpu.VMEM((3, 2, NZ, 64, FF), BF16),
            pltpu.VMEM((3, 64, FF), BF16),
            dma((9, NE)),
            dma((9, NE)),
            dma((2, NZ // GROUP, NE)),
            dma((2, NZ // GROUP, NE)),
            dma((3, 2, NZ)),
            dma((3, 2, NZ)),
            dma((3, 2, NZ - 1)),
            dma((3, 2, NZ - 1)),
            dma((3,)),
            dma((3,)),
        ],
        compiler_params=pltpu.CompilerParams(
            collective_id=0, has_side_effects=True, vmem_limit_bytes=56 * 2**20
        ),
        cost_estimate=pl.CostEstimate(
            flops=9 * 2 * ROWS * WIDE * FF, bytes_accessed=12 * 2**20, transcendentals=ROWS * FF
        ),
        name="moe_layer",
    )(slot_map, live, routes, probs, tokens, cotangent, wg, wu, wd)
    return pl.pallas_call(
        hand_over,
        out_shape=shapes,
        in_specs=[vmem] * 5,
        out_specs=[vmem] * 5,
        name="hand_over",
    )(*results)


def shards(tokens, cotangent, probs, routes, live, slot_map, w_gate, w_up, w_down):
    input_grad, prob_grad, down_share, gate_share, up_share = layer(
        slot_map,
        live,
        routes.T,
        probs.T,
        tokens,
        cotangent,
        w_gate[0],
        w_up[0],
        w_down[0],
    )
    return (
        input_grad,
        prob_grad.T,
        gate_share[None],
        up_share[None],
        down_share.T[None],
    )


def solution(mesh):
    tok = P(("dp", "expert"), None)
    return jax.shard_map(
        shards,
        mesh=mesh,
        in_specs=(
            tok, tok, tok, tok,
            P(("dp", "expert")),
            P(),
            P("expert", None, None),
            P("expert", None, None),
            P("expert", None, None),
        ),
        out_specs=(
            tok,
            tok,
            P("expert", "dp", None),
            P("expert", "dp", None),
            P("expert", None, "dp"),
        ),
        check_vma=False,
    )
```

```python
import jax
import jax.numpy as jnp
from jax import lax
from jax.experimental import pallas as pl
from jax.experimental.pallas import tpu as pltpu
from jax.sharding import PartitionSpec as P

MESH = pl.DeviceIdType.MESH
F32, BF16 = jnp.float32, jnp.bfloat16
NZ = 8
NE = 8
TOK = 128
WIDE = 2048
HALF = 1024
FF = 768
MAIN = 32
REST = 8
ROWS = NE * (MAIN + REST)
LAST = NZ - 1
GROUP = 2
ROUNDS = NZ // GROUP


def mm(a, b):
    return jnp.dot(a, b, preferred_element_type=F32)


def mm_tn(a, b):
    return lax.dot_general(a, b, (((0,), (0,)), ((), ())), preferred_element_type=F32)


def mm_nt(a, b):
    return lax.dot_general(a, b, (((1,), (1,)), ((), ())), preferred_element_type=F32)


def cols_at(start, size):
    return pl.ds(pl.multiple_of(start, size), size)


def one_hot(hit):
    return jnp.where(hit, 1.0, 0.0).astype(BF16)


def layer_kernel(
    slot_ref, live_ref, routes_ref, probs_ref, tok_hbm, cot_hbm, wg_hbm, wu_hbm, wd_hbm,
    in_ref, pg_ref, o_down, o_gate, o_up,
    tok_ref, cot_ref, wg, wu, wd, w_sem,
    pick, pick_a, pick_b, pick48,
    sx, sxt, sdy, sdyt, sp, x, xt, dy, dyt, prob, turned,
    hid, phid, act1, act2, dyw, gg, ug,
    pair, pairt, sbp, back, backt, bp,
    grads, sib, ring, xbuf,
    a2a_s, a2a_r, dy_s, dy_r, sib_s, sib_r, ring_s, ring_r, x_s, x_r,
):
    dp = lax.axis_index("dp")
    me = lax.axis_index("expert")
    xh, z, c = dp // 16, (dp // 2) % NZ, dp % 2
    up = (xh * 16 + ((z + 1) % NZ) * 2 + c, me)
    down = (xh * 16 + ((z + NZ - 1) % NZ) * 2 + c, me)
    sibling = (xh * 16 + z * 2 + (1 - c), me)
    across = ((1 - xh) * 16 + z * 2 + c, me)

    loads = [
        pltpu.make_async_copy(src, dst, w_sem.at[i])
        for i, (src, dst) in enumerate(
            (
                (tok_hbm, tok_ref),
                (cot_hbm, cot_ref),
                (wg_hbm, wg),
                (wu_hbm, wu),
                (wd_hbm, wd),
            )
        )
    ]
    loads[0].start()

    def partner(k):
        return ((me // 4 + 1 - k // 4) % 2) * 4 + (me % 4 + k % 4 + k // 4) % 4

    barrier = pltpu.get_barrier_semaphore()
    for peer in (up, down, sibling, across):
        pl.semaphore_signal(barrier, inc=1, device_id=peer, device_id_type=MESH)
    for k in range(NE - 1):
        pl.semaphore_signal(
            barrier, inc=1, device_id=(dp, partner(k)), device_id_type=MESH
        )
    for load in loads[1:]:
        load.start()

    slot_iota = lax.broadcasted_iota(jnp.int32, (NE, TOK), 0)
    lane = lax.broadcasted_iota(jnp.int32, (1, TOK), 1)
    alive = jnp.where(lane < TOK // 2, live_ref[0], live_ref[1]) == 1
    owners = []
    for k in range(2):
        r = routes_ref[k : k + 1, :]
        o = jnp.zeros((1, TOK), jnp.int32)
        for e in range(NE):
            o = jnp.where(r == e, slot_ref[e], o)
        owners.append(jnp.where(alive, o, -1))
    taken = sum(jnp.where(slot_iota == o, 1.0, 0.0) for o in owners).astype(BF16)
    earlier = lax.broadcasted_iota(jnp.int32, (TOK, TOK), 0) < lax.broadcasted_iota(
        jnp.int32, (TOK, TOK), 1
    )
    before = mm(taken, one_hot(earlier))
    mains, rests, alls = [], [], []
    for o in owners:
        pos = jnp.sum(jnp.where(slot_iota == o, before, 0.0), 0, keepdims=True).astype(jnp.int32)
        mains.append(jnp.where((o >= 0) & (pos < MAIN), o * MAIN + pos, -1))
        rests.append(jnp.where((o >= 0) & (pos >= MAIN), o * 2 * REST + pos - MAIN, -1))
        alls.append(jnp.where(o >= 0, o * 48 + pos, -1))
    row = lax.broadcasted_iota(jnp.int32, (NE * MAIN, TOK), 0)
    pick[...] = one_hot((row == mains[0]) | (row == mains[1]))
    row = lax.broadcasted_iota(jnp.int32, (NE * 2 * REST, TOK), 0)
    pick_a[...] = one_hot((row == rests[0]) | (row == rests[1]))
    low = row - REST
    pick_b[...] = one_hot(
        ((low == rests[0]) & (rests[0] >= 0)) | ((low == rests[1]) & (rests[1] >= 0))
    )

    def dispatch():
        @pl.loop(0, 4)
        def _(n):
            cols = cols_at(n * 512, 512)
            sx[:, cols] = mm(pick[...], tok_ref[:, cols]).astype(BF16)

        @pl.loop(0, 2)
        def _(n):
            cols = cols_at(n * 512, 512)
            more = cols_at(HALF + n * 512, 512)
            sxt[:, cols] = (
                mm(pick_a[...], tok_ref[:, cols]) + mm(pick_b[...], tok_ref[:, more])
            ).astype(BF16)

    def chunk(d, s):
        r, short = s // 2, s % 2
        ahead = (4 - r) * (1 - short) + (5 + r) * short
        return (z + ahead) % NZ if d == 0 else (z + 2 * NZ - ahead) % NZ

    def step_cols(s):
        return cols_at(chunk(0, s) * 128, 128), cols_at(HALF + chunk(1, s) * 128, 128)

    def both(ref, s):
        a, b = step_cols(s)
        return jnp.concatenate([ref[:, a], ref[:, b]], 1)

    def dispatch_cot():
        @pl.loop(0, NZ)
        def _(s):
            a, b = step_cols(s)
            sdy[s] = mm(pick[...], both(cot_ref, s)).astype(BF16)
            sdyt[s] = (mm(pick_a[...], cot_ref[:, a]) + mm(pick_b[...], cot_ref[:, b])).astype(
                BF16
            )

    def piece(ref, kind, e):
        if kind % 3 == 0:
            return ref.at[pl.ds(pl.multiple_of(e * MAIN, MAIN), MAIN)]
        if kind % 3 == 1:
            return ref.at[pl.ds(pl.multiple_of(e * 2 * REST, 2 * REST), 2 * REST)]
        return ref.at[e]

    exchanged = (
        (sx, x), (sxt, xt), (sp, prob),
        None, None, None,
        (pair, back), (pairt, backt), (sbp, bp),
    )

    def exchange(kind, k):
        src, dst = exchanged[kind]
        to = partner(k)
        return pltpu.make_async_remote_copy(
            src_ref=piece(src, kind, to),
            dst_ref=piece(dst, kind, me),
            send_sem=a2a_s.at[kind, k],
            recv_sem=a2a_r.at[kind, k],
            device_id=(dp, to),
            device_id_type=MESH,
        )

    def start_all(kinds):
        @pl.loop(0, NE - 1)
        def _(k):
            for kind in kinds:
                exchange(kind, k).start()

    def keep_own(kinds):
        for kind in kinds:
            src, dst = exchanged[kind]
            if kind % 3 == 2:
                dst[me] = src[me]
            else:
                size = MAIN if kind % 3 == 0 else 2 * REST
                rows = pl.ds(pl.multiple_of(me * size, size), size)
                dst[rows, :] = src[rows, :]

    def wait_sent(kinds):
        @pl.loop(0, NE - 1)
        def _(k):
            for kind in kinds:
                exchange(kind, k).wait_send()

    def wait_got(kinds):
        @pl.loop(0, NE - 1)
        def _(k):
            for kind in kinds:
                exchange(kind, k).wait_recv()

    def dy_copy(kind, g, k):
        to = partner(k)
        steps = pl.ds(g * GROUP, GROUP)
        src, dst, size = ((sdy, dy, MAIN), (sdyt, dyt, 2 * REST))[kind]
        return pltpu.make_async_remote_copy(
            src_ref=src.at[steps, pl.ds(pl.multiple_of(to * size, size), size)],
            dst_ref=dst.at[steps, pl.ds(pl.multiple_of(me * size, size), size)],
            send_sem=dy_s.at[kind, g, k],
            recv_sem=dy_r.at[kind, g, k],
            device_id=(dp, to),
            device_id_type=MESH,
        )

    loads[0].wait()
    dispatch()
    pl.semaphore_wait(barrier, 4 + NE - 1)
    start_all((0, 1))
    row = lax.broadcasted_iota(jnp.int32, (NE * 48, TOK), 0)
    total = jnp.zeros((NE * 48, 1), F32)
    for k in range(2):
        hit = jnp.where(row == alls[k], 1.0, 0.0)
        pick48[k] = hit
        total += jnp.sum(hit * probs_ref[k : k + 1, :].astype(F32), 1, keepdims=True)
    sp[...] = jnp.broadcast_to(total, (NE * 48, 128)).astype(BF16).reshape(NE, 48, 128)
    keep_own((0, 1, 2))
    loads[1].wait()
    dispatch_cot()
    for size, src, dst in ((MAIN, sdy, dy), (2 * REST, sdyt, dyt)):
        rows = pl.ds(pl.multiple_of(me * size, size), size)
        dst[:, rows, :] = src[:, rows, :]
    start_all((2,))

    @pl.loop(0, ROUNDS)
    def _(g):
        @pl.loop(0, NE - 1)
        def _(k):
            for kind in range(2):
                dy_copy(kind, g, k).start()

    part = lax.broadcasted_iota(jnp.int32, (NE * REST, NE * 2 * REST), 0)
    from_row = lax.broadcasted_iota(jnp.int32, (NE * REST, NE * 2 * REST), 1)
    first = (part // REST) * 2 * REST + part % REST
    take_a, take_b = one_hot(from_row == first), one_hot(from_row == first + REST)

    rest_rows = pl.ds(NE * MAIN, NE * REST)
    wait_got((0, 1))

    @pl.loop(0, 2)
    def _(n):
        cols = cols_at(n * 512, 512)
        half = xt[:, cols]
        x[rest_rows, cols] = mm(take_a, half).astype(BF16)
        x[rest_rows, cols_at(HALF + n * 512, 512)] = mm(take_b, half).astype(BF16)

    loads[2].wait()
    loads[3].wait()

    @pl.loop(0, FF // 256)
    def _(n):
        cols = cols_at(n * 256, 256)
        gate = mm(x[...], wg[:, cols])
        u = mm(x[...], wu[:, cols])
        sig = jax.nn.sigmoid(gate)
        gs = gate * sig
        hid[:, cols] = (gs * u).astype(BF16)
        act1[:, cols] = u * sig * (1.0 + gate * (1.0 - sig))
        act2[:, cols] = gs

    loads[4].wait()
    wait_got((2,))
    p_all = prob[...].astype(F32)
    weight = jnp.concatenate(
        [
            p_all[:, :MAIN].reshape(NE * MAIN, 128),
            p_all[:, MAIN : MAIN + REST].reshape(NE * REST, 128),
        ],
        0,
    )[:, :1]
    phid[...] = (weight * hid[...].astype(F32)).astype(BF16)

    def sib_copy(m, d, s):
        at = chunk(d, s)
        return pltpu.make_async_remote_copy(
            src_ref=grads.at[m, d, at, 1 - c],
            dst_ref=sib.at[m, d, at],
            send_sem=sib_s.at[m, d, s],
            recv_sem=sib_r.at[m, d, s],
            device_id=sibling,
            device_id_type=MESH,
        )

    def toward(d, short):
        return up if d == short else down

    def ring_copy(m, d, short, r):
        return pltpu.make_async_remote_copy(
            src_ref=ring.at[m, d, short, r],
            dst_ref=ring.at[m, d, short, r + 1],
            send_sem=ring_s.at[m, d, short, r],
            recv_sem=ring_r.at[m, d, short, r],
            device_id=toward(d, short),
            device_id_type=MESH,
        )

    def x_copy(m):
        return pltpu.make_async_remote_copy(
            src_ref=ring.at[m, 1 - xh, 0, ROUNDS],
            dst_ref=xbuf.at[m],
            send_sem=x_s.at[m],
            recv_sem=x_r.at[m],
            device_id=across,
            device_id_type=MESH,
        )

    def flows(r):
        return [(d, short) for short in range(2 if r < ROUNDS - 1 else 1) for d in range(2)]

    def own(m, d, at):
        return grads[m, d, at, c].astype(F32) + sib[m, d, at].astype(F32)

    def put_grads(m, s, out):
        for d in range(2):
            grads[m, d, chunk(d, s)] = out[d * 128 : d * 128 + 128].reshape(2, 64, FF)
            sib_copy(m, d, s).start()

    def ring_step(m, r):
        for d, short in flows(r):
            s = 2 * r + short
            sib_copy(m, d, s).wait()
            term = own(m, d, chunk(d, s))
            if r > 0:
                ring_copy(m, d, short, r - 1).wait()
                term += ring[m, d, short, r].astype(F32)
            ring[m, d, short, r] = term.astype(BF16)
            ring_copy(m, d, short, r).start()

    def ring_total(m, d):
        return (
            ring[m, d, 0, ROUNDS].astype(F32) + ring[m, d, 1, ROUNDS - 1].astype(F32) + own(m, d, z)
        )

    def ring_end(m):
        for d in range(2):
            sib_copy(m, d, LAST).wait()
            ring_copy(m, d, 0, ROUNDS - 1).wait()
            ring_copy(m, d, 1, ROUNDS - 2).wait()
        ring[m, 1 - xh, 0, ROUNDS] = ring_total(m, 1 - xh).astype(BF16)
        x_copy(m).start()

    dyw[...] = jnp.zeros_like(dyw)
    for g in range(ROUNDS):

        @pl.loop(0, NE - 1)
        def _(k):
            for kind in range(2):
                dy_copy(kind, g, k).wait_recv()

        @pl.loop(g * GROUP, g * GROUP + GROUP)
        def _(s):
            half = dyt[s]
            dy[s, rest_rows, :128] = mm(take_a, half).astype(BF16)
            dy[s, rest_rows, 128:] = mm(take_b, half).astype(BF16)
            put_grads(0, s, mm_tn(dy[s], phid[...]).astype(BF16))

        @pl.loop(g * GROUP, g * GROUP + GROUP)
        def _(s):
            dyw[...] += mm_nt(dy[s], both(wd, s))
            turned[s] = both(x, s).T

        if g < ROUNDS - 1:
            ring_step(0, g)

    total = jnp.zeros((ROWS, 1), F32)
    for n in range(FF // 256):
        cols = pl.ds(n * 256, 256)
        part = dyw[:, cols]
        total += jnp.sum(hid[:, cols].astype(F32) * part, 1, keepdims=True)
        hg = part * weight
        gg[:, cols] = (hg * act1[:, cols]).astype(BF16)
        ug[:, cols] = (hg * act2[:, cols]).astype(BF16)

    for m, right in ((1, gg), (2, ug)):

        @pl.loop(0, NZ)
        def _(s):
            put_grads(m, s, mm(turned[s], right[...]).astype(BF16))

        ring_step(m, 0)
        if m == 1:
            ring_step(0, ROUNDS - 1)

    def pair_cols(n):
        cols = cols_at(n * 256, 256)
        pair[:, cols] = (mm_nt(gg[...], wg[cols, :]) + mm_nt(ug[...], wu[cols, :])).astype(BF16)

    pl.loop(0, 8)(pair_cols)

    @pl.loop(0, 2)
    def _(n):
        cols = cols_at(n * 512, 512)
        pairt[:, cols] = (
            mm_tn(take_a, pair[rest_rows, cols])
            + mm_tn(take_b, pair[rest_rows, cols_at(HALF + n * 512, 512)])
        ).astype(BF16)

    part = jnp.broadcast_to(total, (ROWS, 128))
    sbp[:, :MAIN] = part[: NE * MAIN].reshape(NE, MAIN, 128).astype(BF16)
    sbp[:, MAIN:] = jnp.concatenate(
        [part[NE * MAIN :].reshape(NE, REST, 128), jnp.zeros((NE, REST, 128), F32)], 1
    ).astype(BF16)
    start_all((6, 7, 8))
    keep_own((6, 7, 8))

    for r in range(1, ROUNDS):
        ring_step(1, r)
        ring_step(2, r)
        if r == 1:
            ring_end(0)

    ring_end(1)
    ring_end(2)
    wait_got((6, 7, 8))

    @pl.loop(0, 2)
    def _(n):
        cols = cols_at(n * 512, 512)
        more = cols_at(HALF + n * 512, 512)
        in_ref[:, cols] = (
            mm_tn(pick[...], back[:, cols]) + mm_tn(pick_a[...], backt[:, cols])
        ).astype(BF16)
        in_ref[:, more] = (
            mm_tn(pick[...], back[:, more]) + mm_tn(pick_b[...], backt[:, cols])
        ).astype(BF16)

    parts = bp[...].astype(F32).reshape(NE * 48, 128)
    for k in range(2):
        pg_ref[k : k + 1, :] = jnp.sum(pick48[k] * parts, 0, keepdims=True).astype(BF16)

    for m, out in enumerate((o_down, o_gate, o_up)):
        x_copy(m).wait()
        out[...] = ring_total(m, xh) + xbuf[m].astype(F32)
    wait_sent((0, 1, 2, 6, 7, 8))

    @pl.loop(0, ROUNDS)
    def _(g):
        @pl.loop(0, NE - 1)
        def _(k):
            for kind in range(2):
                dy_copy(kind, g, k).wait_send()


def hand_over(*refs):
    half = len(refs) // 2
    for src, dst in zip(refs[:half], refs[half:]):
        dst[...] = src[...]


def layer(slot_map, live, routes, probs, tokens, cotangent, wg, wu, wd):
    vmem, smem = pl.BlockSpec(memory_space=pltpu.VMEM), pl.BlockSpec(memory_space=pltpu.SMEM)
    anywhere = pl.BlockSpec(memory_space=pl.ANY)
    dma = pltpu.SemaphoreType.DMA
    shapes = [
        jax.ShapeDtypeStruct((TOK, WIDE), BF16),
        jax.ShapeDtypeStruct((2, TOK), BF16),
    ] + [jax.ShapeDtypeStruct((64, FF), F32)] * 3
    results = pl.pallas_call(
        layer_kernel,
        out_shape=shapes,
        in_specs=[smem, smem, vmem, vmem] + [anywhere] * 5,
        out_specs=[vmem] * 5,
        scratch_shapes=[
            pltpu.VMEM((TOK, WIDE), BF16),
            pltpu.VMEM((TOK, WIDE), BF16),
            pltpu.VMEM((WIDE, FF), BF16),
            pltpu.VMEM((WIDE, FF), BF16),
            pltpu.VMEM((FF, WIDE), BF16),
            dma((5,)),
            pltpu.VMEM((NE * MAIN, TOK), BF16),
            pltpu.VMEM((NE * 2 * REST, TOK), BF16),
            pltpu.VMEM((NE * 2 * REST, TOK), BF16),
            pltpu.VMEM((2, NE * 48, TOK), F32),
            pltpu.VMEM((NE * MAIN, WIDE), BF16),
            pltpu.VMEM((NE * 2 * REST, HALF), BF16),
            pltpu.VMEM((NZ, NE * MAIN, 256), BF16),
            pltpu.VMEM((NZ, NE * 2 * REST, 128), BF16),
            pltpu.VMEM((NE, 48, 128), BF16),
            pltpu.VMEM((ROWS, WIDE), BF16),
            pltpu.VMEM((NE * 2 * REST, HALF), BF16),
            pltpu.VMEM((NZ, ROWS, 256), BF16),
            pltpu.VMEM((NZ, NE * 2 * REST, 128), BF16),
            pltpu.VMEM((NE, 48, 128), BF16),
            pltpu.VMEM((NZ, 256, ROWS), BF16),
            pltpu.VMEM((ROWS, FF), BF16),
            pltpu.VMEM((ROWS, FF), BF16),
            pltpu.VMEM((ROWS, FF), F32),
            pltpu.VMEM((ROWS, FF), F32),
            pltpu.VMEM((ROWS, FF), F32),
            pltpu.VMEM((ROWS, FF), BF16),
            pltpu.VMEM((ROWS, FF), BF16),
            pltpu.VMEM((ROWS, WIDE), BF16),
            pltpu.VMEM((NE * 2 * REST, HALF), BF16),
            pltpu.VMEM((NE, 48, 128), BF16),
            pltpu.VMEM((NE * MAIN, WIDE), BF16),
            pltpu.VMEM((NE * 2 * REST, HALF), BF16),
            pltpu.VMEM((NE, 48, 128), BF16),
            pltpu.VMEM((3, 2, NZ, 2, 64, FF), BF16),
            pltpu.VMEM((3, 2, NZ, 64, FF), BF16),
            pltpu.VMEM((3, 2, 2, ROUNDS + 1, 64, FF), BF16),
            pltpu.VMEM((3, 64, FF), BF16),
            dma((9, NE)),
            dma((9, NE)),
            dma((2, ROUNDS, NE)),
            dma((2, ROUNDS, NE)),
            dma((3, 2, NZ)),
            dma((3, 2, NZ)),
            dma((3, 2, 2, ROUNDS)),
            dma((3, 2, 2, ROUNDS)),
            dma((3,)),
            dma((3,)),
        ],
        compiler_params=pltpu.CompilerParams(
            collective_id=0, has_side_effects=True, vmem_limit_bytes=56 * 2**20
        ),
        cost_estimate=pl.CostEstimate(
            flops=9 * 2 * ROWS * WIDE * FF, bytes_accessed=12 * 2**20, transcendentals=ROWS * FF
        ),
        name="moe_layer",
    )(slot_map, live, routes, probs, tokens, cotangent, wg, wu, wd)
    return pl.pallas_call(
        hand_over,
        out_shape=shapes,
        in_specs=[vmem] * 5,
        out_specs=[vmem] * 5,
        name="hand_over",
    )(*results)


def shards(tokens, cotangent, probs, routes, live, slot_map, w_gate, w_up, w_down):
    input_grad, prob_grad, down_share, gate_share, up_share = layer(
        slot_map,
        live,
        routes.T,
        probs.T,
        tokens,
        cotangent,
        w_gate[0],
        w_up[0],
        w_down[0],
    )
    return (
        input_grad,
        prob_grad.T,
        gate_share[None],
        up_share[None],
        down_share.T[None],
    )


def solution(mesh):
    tok = P(("dp", "expert"), None)
    return jax.shard_map(
        shards,
        mesh=mesh,
        in_specs=(
            tok, tok, tok, tok,
            P(("dp", "expert")),
            P(),
            P("expert", None, None),
            P("expert", None, None),
            P("expert", None, None),
        ),
        out_specs=(
            tok,
            tok,
            P("expert", "dp", None),
            P("expert", "dp", None),
            P("expert", None, "dp"),
        ),
        check_vma=False,
    )
```

```python
import jax
import jax.numpy as jnp
from jax import lax
from jax.experimental import pallas as pl
from jax.experimental.pallas import tpu as pltpu
from jax.sharding import PartitionSpec as P

MESH = pl.DeviceIdType.MESH
F32, BF16 = jnp.float32, jnp.bfloat16
NZ = 8
NE = 8
TOK = 128
WIDE = 2048
HALF = 1024
FF = 768
MAIN = 32
REST = 8
ROWS = NE * (MAIN + REST)
LAST = NZ - 1
GROUP = 2
ROUNDS = NZ // GROUP


def mm(a, b):
    return jnp.dot(a, b, preferred_element_type=F32)


def mm_tn(a, b):
    return lax.dot_general(a, b, (((0,), (0,)), ((), ())), preferred_element_type=F32)


def mm_nt(a, b):
    return lax.dot_general(a, b, (((1,), (1,)), ((), ())), preferred_element_type=F32)


def cols_at(start, size):
    return pl.ds(pl.multiple_of(start, size), size)


def one_hot(hit):
    return jnp.where(hit, 1.0, 0.0).astype(BF16)


def layer_kernel(
    slot_hbm, live_hbm, routes_hbm, probs_hbm, tok_hbm, cot_hbm, wg_hbm, wu_hbm, wd_hbm,
    in_out, pg_out, down_out, gate_out, up_out,
    in_ref, pg_ref, o_down, o_gate, o_up, out_sem,
    slot_ref, live_ref, routes_ref, probs_ref, small_sem,
    tok_ref, cot_ref, wg, wu, wd, w_sem,
    pick, pick_a, pick_b, pick48,
    sx, sxt, sdy, sdyt, sp, x, xt, dy, dyt, prob, turned,
    hid, phid, act1, act2, dyw, gg, ug,
    pair, pairt, sbp, back, backt, bp,
    grads, sib, ring, xbuf,
    a2a_s, a2a_r, dy_s, dy_r, sib_s, sib_r, ring_s, ring_r, x_s, x_r,
):
    dp = lax.axis_index("dp")
    me = lax.axis_index("expert")
    xh, z, c = dp // 16, (dp // 2) % NZ, dp % 2
    up = (xh * 16 + ((z + 1) % NZ) * 2 + c, me)
    down = (xh * 16 + ((z + NZ - 1) % NZ) * 2 + c, me)
    sibling = (xh * 16 + z * 2 + (1 - c), me)
    across = ((1 - xh) * 16 + z * 2 + c, me)

    loads = [
        pltpu.make_async_copy(src, dst, w_sem.at[i])
        for i, (src, dst) in enumerate(
            (
                (tok_hbm, tok_ref),
                (cot_hbm, cot_ref),
                (wg_hbm, wg),
                (wu_hbm, wu),
                (wd_hbm, wd),
            )
        )
    ]
    small = [
        pltpu.make_async_copy(src, dst, small_sem.at[i])
        for i, (src, dst) in enumerate(
            (
                (slot_hbm, slot_ref),
                (live_hbm, live_ref),
                (routes_hbm, routes_ref),
                (probs_hbm, probs_ref),
            )
        )
    ]
    for load in small:
        load.start()
    loads[0].start()


    def partner(k):
        return ((me // 4 + 1 - k // 4) % 2) * 4 + (me % 4 + k % 4 + k // 4) % 4

    barrier = pltpu.get_barrier_semaphore()
    for peer in (up, down, sibling, across):
        pl.semaphore_signal(barrier, inc=1, device_id=peer, device_id_type=MESH)
    for k in range(NE - 1):
        pl.semaphore_signal(
            barrier, inc=1, device_id=(dp, partner(k)), device_id_type=MESH
        )
    for load in loads[1:]:
        load.start()
    for load in small:
        load.wait()

    slot_iota = lax.broadcasted_iota(jnp.int32, (NE, TOK), 0)
    lane = lax.broadcasted_iota(jnp.int32, (1, TOK), 1)
    alive = jnp.where(lane < TOK // 2, live_ref[0], live_ref[1]) == 1
    owners = []
    for k in range(2):
        r = routes_ref[k : k + 1, :]
        o = jnp.zeros((1, TOK), jnp.int32)
        for e in range(NE):
            o = jnp.where(r == e, slot_ref[e], o)
        owners.append(jnp.where(alive, o, -1))
    taken = sum(jnp.where(slot_iota == o, 1.0, 0.0) for o in owners).astype(BF16)
    earlier = lax.broadcasted_iota(jnp.int32, (TOK, TOK), 0) < lax.broadcasted_iota(
        jnp.int32, (TOK, TOK), 1
    )
    before = mm(taken, one_hot(earlier))
    mains, rests, alls = [], [], []
    for o in owners:
        pos = jnp.sum(jnp.where(slot_iota == o, before, 0.0), 0, keepdims=True).astype(jnp.int32)
        mains.append(jnp.where((o >= 0) & (pos < MAIN), o * MAIN + pos, -1))
        rests.append(jnp.where((o >= 0) & (pos >= MAIN), o * 2 * REST + pos - MAIN, -1))
        alls.append(jnp.where(o >= 0, o * 48 + pos, -1))
    row = lax.broadcasted_iota(jnp.int32, (NE * MAIN, TOK), 0)
    pick[...] = one_hot((row == mains[0]) | (row == mains[1]))
    row = lax.broadcasted_iota(jnp.int32, (NE * 2 * REST, TOK), 0)
    pick_a[...] = one_hot((row == rests[0]) | (row == rests[1]))
    low = row - REST
    pick_b[...] = one_hot(
        ((low == rests[0]) & (rests[0] >= 0)) | ((low == rests[1]) & (rests[1] >= 0))
    )

    def dispatch():
        @pl.loop(0, 4)
        def _(n):
            cols = cols_at(n * 512, 512)
            sx[:, cols] = mm(pick[...], tok_ref[:, cols]).astype(BF16)

        @pl.loop(0, 2)
        def _(n):
            cols = cols_at(n * 512, 512)
            more = cols_at(HALF + n * 512, 512)
            sxt[:, cols] = (
                mm(pick_a[...], tok_ref[:, cols]) + mm(pick_b[...], tok_ref[:, more])
            ).astype(BF16)

    def chunk(d, s):
        r, short = s // 2, s % 2
        ahead = (4 - r) * (1 - short) + (5 + r) * short
        return (z + ahead) % NZ if d == 0 else (z + 2 * NZ - ahead) % NZ

    def step_cols(s):
        return cols_at(chunk(0, s) * 128, 128), cols_at(HALF + chunk(1, s) * 128, 128)

    def both(ref, s):
        a, b = step_cols(s)
        return jnp.concatenate([ref[:, a], ref[:, b]], 1)

    def dispatch_cot():
        @pl.loop(0, NZ)
        def _(s):
            a, b = step_cols(s)
            sdy[s] = mm(pick[...], both(cot_ref, s)).astype(BF16)
            sdyt[s] = (mm(pick_a[...], cot_ref[:, a]) + mm(pick_b[...], cot_ref[:, b])).astype(
                BF16
            )

    def piece(ref, kind, e):
        if kind % 3 == 0:
            return ref.at[pl.ds(pl.multiple_of(e * MAIN, MAIN), MAIN)]
        if kind % 3 == 1:
            return ref.at[pl.ds(pl.multiple_of(e * 2 * REST, 2 * REST), 2 * REST)]
        return ref.at[e]

    exchanged = (
        (sx, x), (sxt, xt), (sp, prob),
        None, None, None,
        (pair, back), (pairt, backt), (sbp, bp),
    )

    def exchange(kind, k):
        src, dst = exchanged[kind]
        to = partner(k)
        return pltpu.make_async_remote_copy(
            src_ref=piece(src, kind, to),
            dst_ref=piece(dst, kind, me),
            send_sem=a2a_s.at[kind, k],
            recv_sem=a2a_r.at[kind, k],
            device_id=(dp, to),
            device_id_type=MESH,
        )

    def start_all(kinds):
        @pl.loop(0, NE - 1)
        def _(k):
            for kind in kinds:
                exchange(kind, k).start()

    def keep_own(kinds):
        for kind in kinds:
            src, dst = exchanged[kind]
            if kind % 3 == 2:
                dst[me] = src[me]
            else:
                size = MAIN if kind % 3 == 0 else 2 * REST
                rows = pl.ds(pl.multiple_of(me * size, size), size)
                dst[rows, :] = src[rows, :]

    def wait_sent(kinds):
        @pl.loop(0, NE - 1)
        def _(k):
            for kind in kinds:
                exchange(kind, k).wait_send()

    def wait_got(kinds):
        @pl.loop(0, NE - 1)
        def _(k):
            for kind in kinds:
                exchange(kind, k).wait_recv()

    def dy_copy(kind, g, k):
        to = partner(k)
        steps = pl.ds(g * GROUP, GROUP)
        src, dst, size = ((sdy, dy, MAIN), (sdyt, dyt, 2 * REST))[kind]
        return pltpu.make_async_remote_copy(
            src_ref=src.at[steps, pl.ds(pl.multiple_of(to * size, size), size)],
            dst_ref=dst.at[steps, pl.ds(pl.multiple_of(me * size, size), size)],
            send_sem=dy_s.at[kind, g, k],
            recv_sem=dy_r.at[kind, g, k],
            device_id=(dp, to),
            device_id_type=MESH,
        )

    loads[0].wait()
    dispatch()
    pl.semaphore_wait(barrier, 4 + NE - 1)
    start_all((0, 1))
    row = lax.broadcasted_iota(jnp.int32, (NE * 48, TOK), 0)
    total = jnp.zeros((NE * 48, 1), F32)
    for k in range(2):
        hit = jnp.where(row == alls[k], 1.0, 0.0)
        pick48[k] = hit
        total += jnp.sum(hit * probs_ref[k : k + 1, :].astype(F32), 1, keepdims=True)
    sp[...] = jnp.broadcast_to(total, (NE * 48, 128)).astype(BF16).reshape(NE, 48, 128)
    keep_own((0, 1, 2))
    loads[1].wait()
    dispatch_cot()
    for size, src, dst in ((MAIN, sdy, dy), (2 * REST, sdyt, dyt)):
        rows = pl.ds(pl.multiple_of(me * size, size), size)
        dst[:, rows, :] = src[:, rows, :]
    start_all((2,))

    @pl.loop(0, ROUNDS)
    def _(g):
        @pl.loop(0, NE - 1)
        def _(k):
            for kind in range(2):
                dy_copy(kind, g, k).start()

    part = lax.broadcasted_iota(jnp.int32, (NE * REST, NE * 2 * REST), 0)
    from_row = lax.broadcasted_iota(jnp.int32, (NE * REST, NE * 2 * REST), 1)
    first = (part // REST) * 2 * REST + part % REST
    take_a, take_b = one_hot(from_row == first), one_hot(from_row == first + REST)

    rest_rows = pl.ds(NE * MAIN, NE * REST)
    wait_got((0, 1))

    @pl.loop(0, 2)
    def _(n):
        cols = cols_at(n * 512, 512)
        half = xt[:, cols]
        x[rest_rows, cols] = mm(take_a, half).astype(BF16)
        x[rest_rows, cols_at(HALF + n * 512, 512)] = mm(take_b, half).astype(BF16)

    loads[2].wait()
    loads[3].wait()

    @pl.loop(0, FF // 256)
    def _(n):
        cols = cols_at(n * 256, 256)
        gate = mm(x[...], wg[:, cols])
        u = mm(x[...], wu[:, cols])
        sig = jax.nn.sigmoid(gate)
        gs = gate * sig
        hid[:, cols] = (gs * u).astype(BF16)
        act1[:, cols] = u * sig * (1.0 + gate * (1.0 - sig))
        act2[:, cols] = gs

    loads[4].wait()
    wait_got((2,))
    p_all = prob[...].astype(F32)
    weight = jnp.concatenate(
        [
            p_all[:, :MAIN].reshape(NE * MAIN, 128),
            p_all[:, MAIN : MAIN + REST].reshape(NE * REST, 128),
        ],
        0,
    )[:, :1]
    phid[...] = (weight * hid[...].astype(F32)).astype(BF16)

    def sib_copy(m, d, s):
        at = chunk(d, s)
        return pltpu.make_async_remote_copy(
            src_ref=grads.at[m, d, at, 1 - c],
            dst_ref=sib.at[m, d, at],
            send_sem=sib_s.at[m, d, s],
            recv_sem=sib_r.at[m, d, s],
            device_id=sibling,
            device_id_type=MESH,
        )

    def toward(d, short):
        return up if d == short else down

    def ring_copy(m, d, short, r):
        return pltpu.make_async_remote_copy(
            src_ref=ring.at[m, d, short, r],
            dst_ref=ring.at[m, d, short, r + 1],
            send_sem=ring_s.at[m, d, short, r],
            recv_sem=ring_r.at[m, d, short, r],
            device_id=toward(d, short),
            device_id_type=MESH,
        )

    def x_copy(m):
        return pltpu.make_async_remote_copy(
            src_ref=ring.at[m, 1 - xh, 0, ROUNDS],
            dst_ref=xbuf.at[m],
            send_sem=x_s.at[m],
            recv_sem=x_r.at[m],
            device_id=across,
            device_id_type=MESH,
        )

    def flows(r):
        return [(d, short) for short in range(2 if r < ROUNDS - 1 else 1) for d in range(2)]

    def own(m, d, at):
        return grads[m, d, at, c].astype(F32) + sib[m, d, at].astype(F32)

    def put_grads(m, s, out):
        for d in range(2):
            grads[m, d, chunk(d, s)] = out[d * 128 : d * 128 + 128].reshape(2, 64, FF)
            sib_copy(m, d, s).start()

    def ring_step(m, r):
        for d, short in flows(r):
            s = 2 * r + short
            sib_copy(m, d, s).wait()
            term = own(m, d, chunk(d, s))
            if r > 0:
                ring_copy(m, d, short, r - 1).wait()
                term += ring[m, d, short, r].astype(F32)
            ring[m, d, short, r] = term.astype(BF16)
            ring_copy(m, d, short, r).start()

    def ring_total(m, d):
        return (
            ring[m, d, 0, ROUNDS].astype(F32) + ring[m, d, 1, ROUNDS - 1].astype(F32) + own(m, d, z)
        )

    def ring_end(m):
        for d in range(2):
            sib_copy(m, d, LAST).wait()
            ring_copy(m, d, 0, ROUNDS - 1).wait()
            ring_copy(m, d, 1, ROUNDS - 2).wait()
        ring[m, 1 - xh, 0, ROUNDS] = ring_total(m, 1 - xh).astype(BF16)
        x_copy(m).start()

    dyw[...] = jnp.zeros_like(dyw)
    for g in range(ROUNDS):

        @pl.loop(0, NE - 1)
        def _(k):
            for kind in range(2):
                dy_copy(kind, g, k).wait_recv()

        @pl.loop(g * GROUP, g * GROUP + GROUP)
        def _(s):
            half = dyt[s]
            dy[s, rest_rows, :128] = mm(take_a, half).astype(BF16)
            dy[s, rest_rows, 128:] = mm(take_b, half).astype(BF16)
            put_grads(0, s, mm_tn(dy[s], phid[...]).astype(BF16))

        @pl.loop(g * GROUP, g * GROUP + GROUP)
        def _(s):
            dyw[...] += mm_nt(dy[s], both(wd, s))
            turned[s] = both(x, s).T

        if g < ROUNDS - 1:
            ring_step(0, g)

    total = jnp.zeros((ROWS, 1), F32)
    for n in range(FF // 256):
        cols = pl.ds(n * 256, 256)
        part = dyw[:, cols]
        total += jnp.sum(hid[:, cols].astype(F32) * part, 1, keepdims=True)
        hg = part * weight
        gg[:, cols] = (hg * act1[:, cols]).astype(BF16)
        ug[:, cols] = (hg * act2[:, cols]).astype(BF16)

    for m, right in ((1, gg), (2, ug)):

        @pl.loop(0, NZ)
        def _(s):
            put_grads(m, s, mm(turned[s], right[...]).astype(BF16))

        ring_step(m, 0)
        if m == 1:
            ring_step(0, ROUNDS - 1)

    def pair_cols(n):
        cols = cols_at(n * 256, 256)
        pair[:, cols] = (mm_nt(gg[...], wg[cols, :]) + mm_nt(ug[...], wu[cols, :])).astype(BF16)

    pl.loop(0, 8)(pair_cols)

    @pl.loop(0, 2)
    def _(n):
        cols = cols_at(n * 512, 512)
        pairt[:, cols] = (
            mm_tn(take_a, pair[rest_rows, cols])
            + mm_tn(take_b, pair[rest_rows, cols_at(HALF + n * 512, 512)])
        ).astype(BF16)

    part = jnp.broadcast_to(total, (ROWS, 128))
    sbp[:, :MAIN] = part[: NE * MAIN].reshape(NE, MAIN, 128).astype(BF16)
    sbp[:, MAIN:] = jnp.concatenate(
        [part[NE * MAIN :].reshape(NE, REST, 128), jnp.zeros((NE, REST, 128), F32)], 1
    ).astype(BF16)
    start_all((6, 7, 8))
    keep_own((6, 7, 8))

    for r in range(1, ROUNDS):
        ring_step(1, r)
        ring_step(2, r)
        if r == 1:
            ring_end(0)

    results = [
        pltpu.make_async_copy(src, dst, out_sem.at[i])
        for i, (src, dst) in enumerate(
            (
                (o_down, down_out),
                (o_gate, gate_out),
                (o_up, up_out),
                (in_ref, in_out),
                (pg_ref, pg_out),
            )
        )
    ]
    ring_end(1)
    ring_end(2)
    wait_got((6, 7, 8))

    @pl.loop(0, 2)
    def _(n):
        cols = cols_at(n * 512, 512)
        more = cols_at(HALF + n * 512, 512)
        in_ref[:, cols] = (
            mm_tn(pick[...], back[:, cols]) + mm_tn(pick_a[...], backt[:, cols])
        ).astype(BF16)
        in_ref[:, more] = (
            mm_tn(pick[...], back[:, more]) + mm_tn(pick_b[...], backt[:, cols])
        ).astype(BF16)

    parts = bp[...].astype(F32).reshape(NE * 48, 128)
    for k in range(2):
        pg_ref[k : k + 1, :] = jnp.sum(pick48[k] * parts, 0, keepdims=True).astype(BF16)

    results[3].start()
    results[4].start()
    for m, out in enumerate((o_down, o_gate, o_up)):
        x_copy(m).wait()
        out[...] = ring_total(m, xh) + xbuf[m].astype(F32)
        results[m].start()
    for result in results:
        result.wait()
    wait_sent((0, 1, 2, 6, 7, 8))

    @pl.loop(0, ROUNDS)
    def _(g):
        @pl.loop(0, NE - 1)
        def _(k):
            for kind in range(2):
                dy_copy(kind, g, k).wait_send()


def hand_over(*refs):
    srcs, dsts, held, sems = refs[:5], refs[5:10], refs[10:15], refs[15]
    loads = [pltpu.make_async_copy(a, b, sems.at[0, i]) for i, (a, b) in enumerate(zip(srcs, held))]
    stores = [pltpu.make_async_copy(a, b, sems.at[1, i]) for i, (a, b) in enumerate(zip(held, dsts))]
    for load in loads:
        load.start()
    for load, store in zip(loads, stores):
        load.wait()
        store.start()
    for store in stores:
        store.wait()


def layer(slot_map, live, routes, probs, tokens, cotangent, wg, wu, wd):
    anywhere = pl.BlockSpec(memory_space=pl.ANY)
    dma = pltpu.SemaphoreType.DMA
    shapes = [
        jax.ShapeDtypeStruct((TOK, WIDE), BF16),
        jax.ShapeDtypeStruct((2, TOK), BF16),
    ] + [jax.ShapeDtypeStruct((64, FF), F32)] * 3
    results = pl.pallas_call(
        layer_kernel,
        out_shape=shapes,
        in_specs=[anywhere] * 9,
        out_specs=[anywhere] * 5,
        scratch_shapes=[pltpu.VMEM(shape.shape, shape.dtype) for shape in shapes]
        + [
            dma((5,)),
            pltpu.SMEM((NE,), jnp.int32),
            pltpu.SMEM((2,), jnp.int32),
            pltpu.VMEM((2, TOK), jnp.int32),
            pltpu.VMEM((2, TOK), BF16),
            dma((4,)),
            pltpu.VMEM((TOK, WIDE), BF16),
            pltpu.VMEM((TOK, WIDE), BF16),
            pltpu.VMEM((WIDE, FF), BF16),
            pltpu.VMEM((WIDE, FF), BF16),
            pltpu.VMEM((FF, WIDE), BF16),
            dma((5,)),
            pltpu.VMEM((NE * MAIN, TOK), BF16),
            pltpu.VMEM((NE * 2 * REST, TOK), BF16),
            pltpu.VMEM((NE * 2 * REST, TOK), BF16),
            pltpu.VMEM((2, NE * 48, TOK), F32),
            pltpu.VMEM((NE * MAIN, WIDE), BF16),
            pltpu.VMEM((NE * 2 * REST, HALF), BF16),
            pltpu.VMEM((NZ, NE * MAIN, 256), BF16),
            pltpu.VMEM((NZ, NE * 2 * REST, 128), BF16),
            pltpu.VMEM((NE, 48, 128), BF16),
            pltpu.VMEM((ROWS, WIDE), BF16),
            pltpu.VMEM((NE * 2 * REST, HALF), BF16),
            pltpu.VMEM((NZ, ROWS, 256), BF16),
            pltpu.VMEM((NZ, NE * 2 * REST, 128), BF16),
            pltpu.VMEM((NE, 48, 128), BF16),
            pltpu.VMEM((NZ, 256, ROWS), BF16),
            pltpu.VMEM((ROWS, FF), BF16),
            pltpu.VMEM((ROWS, FF), BF16),
            pltpu.VMEM((ROWS, FF), F32),
            pltpu.VMEM((ROWS, FF), F32),
            pltpu.VMEM((ROWS, FF), F32),
            pltpu.VMEM((ROWS, FF), BF16),
            pltpu.VMEM((ROWS, FF), BF16),
            pltpu.VMEM((ROWS, WIDE), BF16),
            pltpu.VMEM((NE * 2 * REST, HALF), BF16),
            pltpu.VMEM((NE, 48, 128), BF16),
            pltpu.VMEM((NE * MAIN, WIDE), BF16),
            pltpu.VMEM((NE * 2 * REST, HALF), BF16),
            pltpu.VMEM((NE, 48, 128), BF16),
            pltpu.VMEM((3, 2, NZ, 2, 64, FF), BF16),
            pltpu.VMEM((3, 2, NZ, 64, FF), BF16),
            pltpu.VMEM((3, 2, 2, ROUNDS + 1, 64, FF), BF16),
            pltpu.VMEM((3, 64, FF), BF16),
            dma((9, NE)),
            dma((9, NE)),
            dma((2, ROUNDS, NE)),
            dma((2, ROUNDS, NE)),
            dma((3, 2, NZ)),
            dma((3, 2, NZ)),
            dma((3, 2, 2, ROUNDS)),
            dma((3, 2, 2, ROUNDS)),
            dma((3,)),
            dma((3,)),
        ],
        compiler_params=pltpu.CompilerParams(
            collective_id=0, has_side_effects=True, vmem_limit_bytes=56 * 2**20
        ),
        cost_estimate=pl.CostEstimate(
            flops=9 * 2 * ROWS * WIDE * FF, bytes_accessed=12 * 2**20, transcendentals=ROWS * FF
        ),
        name="moe_layer",
    )(slot_map, live, routes, probs, tokens, cotangent, wg, wu, wd)
    return pl.pallas_call(
        hand_over,
        out_shape=shapes,
        in_specs=[anywhere] * 5,
        out_specs=[anywhere] * 5,
        scratch_shapes=[pltpu.VMEM(shape.shape, shape.dtype) for shape in shapes] + [dma((2, 5))],
        name="hand_over",
    )(*results)


def shards(tokens, cotangent, probs, routes, live, slot_map, w_gate, w_up, w_down):
    input_grad, prob_grad, down_share, gate_share, up_share = layer(
        slot_map,
        live,
        routes.T,
        probs.T,
        tokens,
        cotangent,
        w_gate[0],
        w_up[0],
        w_down[0],
    )
    return (
        input_grad,
        prob_grad.T,
        gate_share[None],
        up_share[None],
        down_share.T[None],
    )


def solution(mesh):
    tok = P(("dp", "expert"), None)
    return jax.shard_map(
        shards,
        mesh=mesh,
        in_specs=(
            tok, tok, tok, tok,
            P(("dp", "expert")),
            P(),
            P("expert", None, None),
            P("expert", None, None),
            P("expert", None, None),
        ),
        out_specs=(
            tok,
            tok,
            P("expert", "dp", None),
            P("expert", "dp", None),
            P("expert", None, "dp"),
        ),
        check_vma=False,
    )
```

```python
import jax
import jax.numpy as jnp
from jax import lax
from jax.experimental import pallas as pl
from jax.experimental.pallas import tpu as pltpu
from jax.sharding import PartitionSpec as P

MESH = pl.DeviceIdType.MESH
F32, BF16 = jnp.float32, jnp.bfloat16
NZ = 8
NE = 8
TOK = 128
WIDE = 2048
HALF = 1024
FF = 768
MAIN = 32
REST = 8
ROWS = NE * (MAIN + REST)
LAST = NZ - 1
GROUP = 2
ROUNDS = NZ // GROUP


def mm(a, b):
    return jnp.dot(a, b, preferred_element_type=F32)


def mm_tn(a, b):
    return lax.dot_general(a, b, (((0,), (0,)), ((), ())), preferred_element_type=F32)


def mm_nt(a, b):
    return lax.dot_general(a, b, (((1,), (1,)), ((), ())), preferred_element_type=F32)


def cols_at(start, size):
    return pl.ds(pl.multiple_of(start, size), size)


def one_hot(hit):
    return jnp.where(hit, 1.0, 0.0).astype(BF16)


def layer_kernel(
    slot_hbm, live_hbm, routes_hbm, probs_hbm, tok_hbm, cot_hbm, wg_hbm, wu_hbm, wd_hbm,
    in_out, pg_out, down_out, gate_out, up_out,
    in_ref, pg_ref, o_down, o_gate, o_up, out_sem,
    slot_ref, live_ref, routes_ref, probs_ref, small_sem,
    tok_ref, cot_ref, wg, wu, wd, w_sem,
    pick, pick_a, pick_b, pick48,
    sx, sxt, sdy, sdyt, sp, x, xt, dy, dyt, prob, turned,
    hid, phid, act1, act2, dyw, gg, ug,
    pair, pairt, sbp, back, backt, bp,
    grads, sib, ring, xbuf,
    a2a_s, a2a_r, dy_s, dy_r, sib_s, sib_r, ring_s, ring_r, x_s, x_r,
):
    dp = lax.axis_index("dp")
    me = lax.axis_index("expert")
    xh, z, c = dp // 16, (dp // 2) % NZ, dp % 2
    up = (xh * 16 + ((z + 1) % NZ) * 2 + c, me)
    down = (xh * 16 + ((z + NZ - 1) % NZ) * 2 + c, me)
    sibling = (xh * 16 + z * 2 + (1 - c), me)
    across = ((1 - xh) * 16 + z * 2 + c, me)

    loads = [
        pltpu.make_async_copy(src, dst, w_sem.at[i])
        for i, (src, dst) in enumerate(
            (
                (tok_hbm, tok_ref),
                (cot_hbm, cot_ref),
                (wg_hbm, wg),
                (wu_hbm, wu),
                (wd_hbm, wd),
            )
        )
    ]
    small = [
        pltpu.make_async_copy(src, dst, small_sem.at[i])
        for i, (src, dst) in enumerate(
            (
                (slot_hbm, slot_ref),
                (live_hbm, live_ref),
                (routes_hbm, routes_ref),
                (probs_hbm, probs_ref),
            )
        )
    ]
    for load in small:
        load.start()
    loads[0].start()


    def partner(k):
        return ((me // 4 + 1 - k // 4) % 2) * 4 + (me % 4 + k % 4 + k // 4) % 4

    barrier = pltpu.get_barrier_semaphore()
    for peer in (up, down, sibling, across):
        pl.semaphore_signal(barrier, inc=1, device_id=peer, device_id_type=MESH)
    for k in range(NE - 1):
        pl.semaphore_signal(
            barrier, inc=1, device_id=(dp, partner(k)), device_id_type=MESH
        )
    for load in loads[1:]:
        load.start()
    for load in small:
        load.wait()

    slot_iota = lax.broadcasted_iota(jnp.int32, (NE, TOK), 0)
    lane = lax.broadcasted_iota(jnp.int32, (1, TOK), 1)
    alive = jnp.where(lane < TOK // 2, live_ref[0], live_ref[1]) == 1
    owners = []
    for k in range(2):
        r = routes_ref[k : k + 1, :]
        o = jnp.zeros((1, TOK), jnp.int32)
        for e in range(NE):
            o = jnp.where(r == e, slot_ref[e], o)
        owners.append(jnp.where(alive, o, -1))
    taken = sum(jnp.where(slot_iota == o, 1.0, 0.0) for o in owners).astype(BF16)
    earlier = lax.broadcasted_iota(jnp.int32, (TOK, TOK), 0) < lax.broadcasted_iota(
        jnp.int32, (TOK, TOK), 1
    )
    before = mm(taken, one_hot(earlier))
    mains, rests, alls = [], [], []
    for o in owners:
        pos = jnp.sum(jnp.where(slot_iota == o, before, 0.0), 0, keepdims=True).astype(jnp.int32)
        mains.append(jnp.where((o >= 0) & (pos < MAIN), o * MAIN + pos, -1))
        rests.append(jnp.where((o >= 0) & (pos >= MAIN), o * 2 * REST + pos - MAIN, -1))
        alls.append(jnp.where(o >= 0, o * 48 + pos, -1))
    row = lax.broadcasted_iota(jnp.int32, (NE * MAIN, TOK), 0)
    pick[...] = one_hot((row == mains[0]) | (row == mains[1]))
    row = lax.broadcasted_iota(jnp.int32, (NE * 2 * REST, TOK), 0)
    pick_a[...] = one_hot((row == rests[0]) | (row == rests[1]))
    low = row - REST
    pick_b[...] = one_hot(
        ((low == rests[0]) & (rests[0] >= 0)) | ((low == rests[1]) & (rests[1] >= 0))
    )

    def dispatch():
        @pl.loop(0, 4)
        def _(n):
            cols = cols_at(n * 512, 512)
            sx[:, cols] = mm(pick[...], tok_ref[:, cols]).astype(BF16)

        @pl.loop(0, 2)
        def _(n):
            cols = cols_at(n * 512, 512)
            more = cols_at(HALF + n * 512, 512)
            sxt[:, cols] = (
                mm(pick_a[...], tok_ref[:, cols]) + mm(pick_b[...], tok_ref[:, more])
            ).astype(BF16)

    def chunk(d, s):
        r, short = s // 2, s % 2
        ahead = (4 - r) * (1 - short) + (5 + r) * short
        return (z + ahead) % NZ if d == 0 else (z + 2 * NZ - ahead) % NZ

    def step_cols(s):
        return cols_at(chunk(0, s) * 128, 128), cols_at(HALF + chunk(1, s) * 128, 128)

    def both(ref, s):
        a, b = step_cols(s)
        return jnp.concatenate([ref[:, a], ref[:, b]], 1)

    def dispatch_cot():
        @pl.loop(0, NZ)
        def _(s):
            a, b = step_cols(s)
            sdy[s] = mm(pick[...], both(cot_ref, s)).astype(BF16)
            sdyt[s] = (mm(pick_a[...], cot_ref[:, a]) + mm(pick_b[...], cot_ref[:, b])).astype(
                BF16
            )

    def piece(ref, kind, e):
        if kind % 3 == 0:
            return ref.at[pl.ds(pl.multiple_of(e * MAIN, MAIN), MAIN)]
        if kind % 3 == 1:
            return ref.at[pl.ds(pl.multiple_of(e * 2 * REST, 2 * REST), 2 * REST)]
        return ref.at[e]

    exchanged = (
        (sx, x), (sxt, xt), (sp, prob),
        None, None, None,
        (pair, back), (pairt, backt), (sbp, bp),
    )

    def exchange(kind, k):
        src, dst = exchanged[kind]
        to = partner(k)
        return pltpu.make_async_remote_copy(
            src_ref=piece(src, kind, to),
            dst_ref=piece(dst, kind, me),
            send_sem=a2a_s.at[kind, k],
            recv_sem=a2a_r.at[kind, k],
            device_id=(dp, to),
            device_id_type=MESH,
        )

    def start_all(kinds):
        @pl.loop(0, NE - 1)
        def _(k):
            for kind in kinds:
                exchange(kind, k).start()

    def keep_own(kinds):
        for kind in kinds:
            src, dst = exchanged[kind]
            if kind % 3 == 2:
                dst[me] = src[me]
            else:
                size = MAIN if kind % 3 == 0 else 2 * REST
                rows = pl.ds(pl.multiple_of(me * size, size), size)
                dst[rows, :] = src[rows, :]

    def wait_sent(kinds):
        @pl.loop(0, NE - 1)
        def _(k):
            for kind in kinds:
                exchange(kind, k).wait_send()

    def wait_got(kinds):
        @pl.loop(0, NE - 1)
        def _(k):
            for kind in kinds:
                exchange(kind, k).wait_recv()

    def dy_copy(kind, g, k):
        to = partner(k)
        steps = pl.ds(g * GROUP, GROUP)
        src, dst, size = ((sdy, dy, MAIN), (sdyt, dyt, 2 * REST))[kind]
        return pltpu.make_async_remote_copy(
            src_ref=src.at[steps, pl.ds(pl.multiple_of(to * size, size), size)],
            dst_ref=dst.at[steps, pl.ds(pl.multiple_of(me * size, size), size)],
            send_sem=dy_s.at[kind, g, k],
            recv_sem=dy_r.at[kind, g, k],
            device_id=(dp, to),
            device_id_type=MESH,
        )

    loads[0].wait()
    dispatch()
    pl.semaphore_wait(barrier, 4 + NE - 1)
    start_all((0, 1))
    row = lax.broadcasted_iota(jnp.int32, (NE * 48, TOK), 0)
    total = jnp.zeros((NE * 48, 1), F32)
    for k in range(2):
        hit = jnp.where(row == alls[k], 1.0, 0.0)
        pick48[k] = hit
        total += jnp.sum(hit * probs_ref[k : k + 1, :].astype(F32), 1, keepdims=True)
    sp[...] = jnp.broadcast_to(total, (NE * 48, 128)).astype(BF16).reshape(NE, 48, 128)
    keep_own((0, 1, 2))
    loads[1].wait()
    dispatch_cot()
    for size, src, dst in ((MAIN, sdy, dy), (2 * REST, sdyt, dyt)):
        rows = pl.ds(pl.multiple_of(me * size, size), size)
        dst[:, rows, :] = src[:, rows, :]
    start_all((2,))

    @pl.loop(0, ROUNDS)
    def _(g):
        @pl.loop(0, NE - 1)
        def _(k):
            for kind in range(2):
                dy_copy(kind, g, k).start()

    part = lax.broadcasted_iota(jnp.int32, (NE * REST, NE * 2 * REST), 0)
    from_row = lax.broadcasted_iota(jnp.int32, (NE * REST, NE * 2 * REST), 1)
    first = (part // REST) * 2 * REST + part % REST
    take_a, take_b = one_hot(from_row == first), one_hot(from_row == first + REST)

    rest_rows = pl.ds(NE * MAIN, NE * REST)
    wait_got((0, 1))

    @pl.loop(0, 2)
    def _(n):
        cols = cols_at(n * 512, 512)
        half = xt[:, cols]
        x[rest_rows, cols] = mm(take_a, half).astype(BF16)
        x[rest_rows, cols_at(HALF + n * 512, 512)] = mm(take_b, half).astype(BF16)

    loads[2].wait()
    loads[3].wait()

    @pl.loop(0, FF // 256)
    def _(n):
        cols = cols_at(n * 256, 256)
        gate = mm(x[...], wg[:, cols])
        u = mm(x[...], wu[:, cols])
        sig = jax.nn.sigmoid(gate)
        gs = gate * sig
        hid[:, cols] = (gs * u).astype(BF16)
        act1[:, cols] = u * sig * (1.0 + gate * (1.0 - sig))
        act2[:, cols] = gs

    loads[4].wait()
    wait_got((2,))
    p_all = prob[...].astype(F32)
    weight = jnp.concatenate(
        [
            p_all[:, :MAIN].reshape(NE * MAIN, 128),
            p_all[:, MAIN : MAIN + REST].reshape(NE * REST, 128),
        ],
        0,
    )[:, :1]
    phid[...] = (weight * hid[...].astype(F32)).astype(BF16)

    def sib_copy(m, d, s):
        at = chunk(d, s)
        return pltpu.make_async_remote_copy(
            src_ref=grads.at[m, d, at, 1 - c],
            dst_ref=sib.at[m, d, at],
            send_sem=sib_s.at[m, d, s],
            recv_sem=sib_r.at[m, d, s],
            device_id=sibling,
            device_id_type=MESH,
        )

    def toward(d, short):
        return up if d == short else down

    def ring_copy(m, d, short, r):
        return pltpu.make_async_remote_copy(
            src_ref=ring.at[m, d, short, r],
            dst_ref=ring.at[m, d, short, r + 1],
            send_sem=ring_s.at[m, d, short, r],
            recv_sem=ring_r.at[m, d, short, r],
            device_id=toward(d, short),
            device_id_type=MESH,
        )

    def x_copy(m):
        return pltpu.make_async_remote_copy(
            src_ref=ring.at[m, 1 - xh, 0, ROUNDS],
            dst_ref=xbuf.at[m],
            send_sem=x_s.at[m],
            recv_sem=x_r.at[m],
            device_id=across,
            device_id_type=MESH,
        )

    def flows(r):
        return [(d, short) for short in range(2 if r < ROUNDS - 1 else 1) for d in range(2)]

    def own(m, d, at):
        return grads[m, d, at, c].astype(F32) + sib[m, d, at].astype(F32)

    def put_grads(m, s, out):
        for d in range(2):
            grads[m, d, chunk(d, s)] = out[d * 128 : d * 128 + 128].reshape(2, 64, FF)
            sib_copy(m, d, s).start()

    def ring_step(m, r):
        for d, short in flows(r):
            s = 2 * r + short
            sib_copy(m, d, s).wait()
            term = own(m, d, chunk(d, s))
            if r > 0:
                ring_copy(m, d, short, r - 1).wait()
                term += ring[m, d, short, r].astype(F32)
            ring[m, d, short, r] = term.astype(BF16)
            ring_copy(m, d, short, r).start()

    def ring_total(m, d):
        return (
            ring[m, d, 0, ROUNDS].astype(F32) + ring[m, d, 1, ROUNDS - 1].astype(F32) + own(m, d, z)
        )

    def ring_end(m):
        for d in range(2):
            sib_copy(m, d, LAST).wait()
            ring_copy(m, d, 0, ROUNDS - 1).wait()
            ring_copy(m, d, 1, ROUNDS - 2).wait()
        ring[m, 1 - xh, 0, ROUNDS] = ring_total(m, 1 - xh).astype(BF16)
        x_copy(m).start()

    dyw[...] = jnp.zeros_like(dyw)
    for g in range(ROUNDS):

        @pl.loop(0, NE - 1)
        def _(k):
            for kind in range(2):
                dy_copy(kind, g, k).wait_recv()

        @pl.loop(g * GROUP, g * GROUP + GROUP)
        def _(s):
            half = dyt[s]
            dy[s, rest_rows, :128] = mm(take_a, half).astype(BF16)
            dy[s, rest_rows, 128:] = mm(take_b, half).astype(BF16)
            put_grads(0, s, mm_tn(dy[s], phid[...]).astype(BF16))

        @pl.loop(g * GROUP, g * GROUP + GROUP)
        def _(s):
            dyw[...] += mm_nt(dy[s], both(wd, s))
            turned[s] = both(x, s).T

        if g < ROUNDS - 1:
            ring_step(0, g)

    total = jnp.zeros((ROWS, 1), F32)
    for n in range(FF // 256):
        cols = pl.ds(n * 256, 256)
        part = dyw[:, cols]
        total += jnp.sum(hid[:, cols].astype(F32) * part, 1, keepdims=True)
        hg = part * weight
        gg[:, cols] = (hg * act1[:, cols]).astype(BF16)
        ug[:, cols] = (hg * act2[:, cols]).astype(BF16)

    def pair_cols(n):
        cols = cols_at(n * 256, 256)
        pair[:, cols] = (mm_nt(gg[...], wg[cols, :]) + mm_nt(ug[...], wu[cols, :])).astype(BF16)

    for m, right in ((1, gg), (2, ug)):

        @pl.loop(0, NZ)
        def _(s):
            put_grads(m, s, mm(turned[s], right[...]).astype(BF16))

        if m == 2:
            pl.loop(0, 2)(pair_cols)
        ring_step(m, 0)
        if m == 1:
            ring_step(0, ROUNDS - 1)

    pl.loop(2, 8)(pair_cols)

    @pl.loop(0, 2)
    def _(n):
        cols = cols_at(n * 512, 512)
        pairt[:, cols] = (
            mm_tn(take_a, pair[rest_rows, cols])
            + mm_tn(take_b, pair[rest_rows, cols_at(HALF + n * 512, 512)])
        ).astype(BF16)

    part = jnp.broadcast_to(total, (ROWS, 128))
    sbp[:, :MAIN] = part[: NE * MAIN].reshape(NE, MAIN, 128).astype(BF16)
    sbp[:, MAIN:] = jnp.concatenate(
        [part[NE * MAIN :].reshape(NE, REST, 128), jnp.zeros((NE, REST, 128), F32)], 1
    ).astype(BF16)
    start_all((6, 7, 8))
    keep_own((6, 7, 8))

    for r in range(1, ROUNDS):
        ring_step(1, r)
        ring_step(2, r)
        if r == 1:
            ring_end(0)

    results = [
        pltpu.make_async_copy(src, dst, out_sem.at[i])
        for i, (src, dst) in enumerate(
            (
                (o_down, down_out),
                (o_gate, gate_out),
                (o_up, up_out),
                (in_ref, in_out),
                (pg_ref, pg_out),
            )
        )
    ]
    ring_end(1)
    ring_end(2)
    wait_got((6, 7, 8))

    @pl.loop(0, 2)
    def _(n):
        cols = cols_at(n * 512, 512)
        more = cols_at(HALF + n * 512, 512)
        in_ref[:, cols] = (
            mm_tn(pick[...], back[:, cols]) + mm_tn(pick_a[...], backt[:, cols])
        ).astype(BF16)
        in_ref[:, more] = (
            mm_tn(pick[...], back[:, more]) + mm_tn(pick_b[...], backt[:, cols])
        ).astype(BF16)

    parts = bp[...].astype(F32).reshape(NE * 48, 128)
    for k in range(2):
        pg_ref[k : k + 1, :] = jnp.sum(pick48[k] * parts, 0, keepdims=True).astype(BF16)

    results[3].start()
    results[4].start()
    for m, out in enumerate((o_down, o_gate, o_up)):
        x_copy(m).wait()
        out[...] = ring_total(m, xh) + xbuf[m].astype(F32)
        results[m].start()
    for result in results:
        result.wait()
    wait_sent((0, 1, 2, 6, 7, 8))

    @pl.loop(0, ROUNDS)
    def _(g):
        @pl.loop(0, NE - 1)
        def _(k):
            for kind in range(2):
                dy_copy(kind, g, k).wait_send()


def hand_over(*refs):
    srcs, dsts, held, sems = refs[:5], refs[5:10], refs[10:15], refs[15]
    loads = [pltpu.make_async_copy(a, b, sems.at[0, i]) for i, (a, b) in enumerate(zip(srcs, held))]
    stores = [pltpu.make_async_copy(a, b, sems.at[1, i]) for i, (a, b) in enumerate(zip(held, dsts))]
    for load in loads:
        load.start()
    for load, store in zip(loads, stores):
        load.wait()
        store.start()
    for store in stores:
        store.wait()


def layer(slot_map, live, routes, probs, tokens, cotangent, wg, wu, wd):
    anywhere = pl.BlockSpec(memory_space=pl.ANY)
    dma = pltpu.SemaphoreType.DMA
    shapes = [
        jax.ShapeDtypeStruct((TOK, WIDE), BF16),
        jax.ShapeDtypeStruct((2, TOK), BF16),
    ] + [jax.ShapeDtypeStruct((64, FF), F32)] * 3
    results = pl.pallas_call(
        layer_kernel,
        out_shape=shapes,
        in_specs=[anywhere] * 9,
        out_specs=[anywhere] * 5,
        scratch_shapes=[pltpu.VMEM(shape.shape, shape.dtype) for shape in shapes]
        + [
            dma((5,)),
            pltpu.SMEM((NE,), jnp.int32),
            pltpu.SMEM((2,), jnp.int32),
            pltpu.VMEM((2, TOK), jnp.int32),
            pltpu.VMEM((2, TOK), BF16),
            dma((4,)),
            pltpu.VMEM((TOK, WIDE), BF16),
            pltpu.VMEM((TOK, WIDE), BF16),
            pltpu.VMEM((WIDE, FF), BF16),
            pltpu.VMEM((WIDE, FF), BF16),
            pltpu.VMEM((FF, WIDE), BF16),
            dma((5,)),
            pltpu.VMEM((NE * MAIN, TOK), BF16),
            pltpu.VMEM((NE * 2 * REST, TOK), BF16),
            pltpu.VMEM((NE * 2 * REST, TOK), BF16),
            pltpu.VMEM((2, NE * 48, TOK), F32),
            pltpu.VMEM((NE * MAIN, WIDE), BF16),
            pltpu.VMEM((NE * 2 * REST, HALF), BF16),
            pltpu.VMEM((NZ, NE * MAIN, 256), BF16),
            pltpu.VMEM((NZ, NE * 2 * REST, 128), BF16),
            pltpu.VMEM((NE, 48, 128), BF16),
            pltpu.VMEM((ROWS, WIDE), BF16),
            pltpu.VMEM((NE * 2 * REST, HALF), BF16),
            pltpu.VMEM((NZ, ROWS, 256), BF16),
            pltpu.VMEM((NZ, NE * 2 * REST, 128), BF16),
            pltpu.VMEM((NE, 48, 128), BF16),
            pltpu.VMEM((NZ, 256, ROWS), BF16),
            pltpu.VMEM((ROWS, FF), BF16),
            pltpu.VMEM((ROWS, FF), BF16),
            pltpu.VMEM((ROWS, FF), F32),
            pltpu.VMEM((ROWS, FF), F32),
            pltpu.VMEM((ROWS, FF), F32),
            pltpu.VMEM((ROWS, FF), BF16),
            pltpu.VMEM((ROWS, FF), BF16),
            pltpu.VMEM((ROWS, WIDE), BF16),
            pltpu.VMEM((NE * 2 * REST, HALF), BF16),
            pltpu.VMEM((NE, 48, 128), BF16),
            pltpu.VMEM((NE * MAIN, WIDE), BF16),
            pltpu.VMEM((NE * 2 * REST, HALF), BF16),
            pltpu.VMEM((NE, 48, 128), BF16),
            pltpu.VMEM((3, 2, NZ, 2, 64, FF), BF16),
            pltpu.VMEM((3, 2, NZ, 64, FF), BF16),
            pltpu.VMEM((3, 2, 2, ROUNDS + 1, 64, FF), BF16),
            pltpu.VMEM((3, 64, FF), BF16),
            dma((9, NE)),
            dma((9, NE)),
            dma((2, ROUNDS, NE)),
            dma((2, ROUNDS, NE)),
            dma((3, 2, NZ)),
            dma((3, 2, NZ)),
            dma((3, 2, 2, ROUNDS)),
            dma((3, 2, 2, ROUNDS)),
            dma((3,)),
            dma((3,)),
        ],
        compiler_params=pltpu.CompilerParams(
            collective_id=0, has_side_effects=True, vmem_limit_bytes=56 * 2**20
        ),
        cost_estimate=pl.CostEstimate(
            flops=9 * 2 * ROWS * WIDE * FF, bytes_accessed=12 * 2**20, transcendentals=ROWS * FF
        ),
        name="moe_layer",
    )(slot_map, live, routes, probs, tokens, cotangent, wg, wu, wd)
    return pl.pallas_call(
        hand_over,
        out_shape=shapes,
        in_specs=[anywhere] * 5,
        out_specs=[anywhere] * 5,
        scratch_shapes=[pltpu.VMEM(shape.shape, shape.dtype) for shape in shapes] + [dma((2, 5))],
        name="hand_over",
    )(*results)


def shards(tokens, cotangent, probs, routes, live, slot_map, w_gate, w_up, w_down):
    input_grad, prob_grad, down_share, gate_share, up_share = layer(
        slot_map,
        live,
        routes.T,
        probs.T,
        tokens,
        cotangent,
        w_gate[0],
        w_up[0],
        w_down[0],
    )
    return (
        input_grad,
        prob_grad.T,
        gate_share[None],
        up_share[None],
        down_share.T[None],
    )


def solution(mesh):
    tok = P(("dp", "expert"), None)
    return jax.shard_map(
        shards,
        mesh=mesh,
        in_specs=(
            tok, tok, tok, tok,
            P(("dp", "expert")),
            P(),
            P("expert", None, None),
            P("expert", None, None),
            P("expert", None, None),
        ),
        out_specs=(
            tok,
            tok,
            P("expert", "dp", None),
            P("expert", "dp", None),
            P("expert", None, "dp"),
        ),
        check_vma=False,
    )
```
